256 devices in a mesh: dp: 2 (over core), fsdp: 4 (over x), tensor: 32 (over z, y).
Axes of the slice: x: 4, y: 4, z: 8, core: 2. Of those that a mesh axis runs over, the one named last changes fastest.
Arguments:
- gradients: bfloat16 [2, 32, 1024, 1024], P('dp', 'fsdp', 'tensor')
- owner_lists: int32 [4, 8], P('fsdp'), may hold values from 0 to 1, as said below
- left_stats: float32 [2, 4, 6, 1024, 1024], P('dp', 'fsdp', None, 'tensor')
- right_stats: float32 [2, 4, 6, 1024, 1024], P('dp', 'fsdp', None, 'tensor')
- left_roots: bfloat16 [2, 4, 6, 1024, 1024], P('dp', 'fsdp', None, 'tensor'), as said below
- right_roots: bfloat16 [2, 4, 6, 1024, 1024], P('dp', 'fsdp', None, 'tensor'), as said below
Outputs:
- new_left: float32 [2, 4, 6, 1024, 1024], P('dp', 'fsdp', None, 'tensor')
- new_right: float32 [2, 4, 6, 1024, 1024], P('dp', 'fsdp', None, 'tensor')
- updates: bfloat16 [32, 1024, 1024], P('fsdp', 'tensor')
The draws below stay inside these ranges and needn't reach their ends.
Inputs may be any that keep to these rules, and one draw needn't show every extreme that they name: `owner_lists`: each index of dp owns at most 6 of the blocks of one index of fsdp, and in every row one index owns exactly 6. Every block of left_roots is symmetric. Every block of right_roots is symmetric.
All inputs are finite; a program needn't handle non-finite values.
Results may differ from the reference program's by a relative error of at most 0.017.
Values may be sent and summed in bfloat16 or wider, within the bound.
A program may use at most 128 MiB of HBM per device.

```python
import math
import jax
import jax.numpy as jnp
from jax import lax

BLOCK = 1024
KF = 8
SLOTS = 6
N_DP = 2
N_FSDP = 4


def draw_gradients(key, part):
    key = jax.random.fold_in(key, 3)
    key_a, key_b, key_c = jax.random.split(key, 3)
    block_total = N_FSDP * KF
    full_shape = (N_DP, block_total, BLOCK, BLOCK)
    block_scale = 4.0 ** (jnp.arange(block_total, dtype=jnp.float32) / max(block_total - 1, 1))
    block_scale = block_scale * jax.random.uniform(key_a, (block_total,), jnp.float32, 1.0, 2.0)
    row_scale = jnp.exp(jax.random.uniform(key_b, (block_total, BLOCK), jnp.float32, 0.0, math.log(10.0)))
    noise_part = jax.random.normal(key_c, full_shape, jnp.float32)
    scaled_noise = noise_part * block_scale[None, :, None, None] * row_scale[None, :, :, None]
    return scaled_noise.astype(jnp.bfloat16)


def owner_row(key):
    key_a, key_b, key_c = jax.random.split(key, 3)
    heavy_owner = jax.random.randint(key_a, (), 0, N_DP)
    other_owners = (heavy_owner + 1 + jnp.arange((N_DP - 1) * SLOTS) // SLOTS) % N_DP
    other_owners = jax.random.permutation(key_b, other_owners)
    listed = jnp.concatenate([jnp.zeros((SLOTS,), jnp.int32) + heavy_owner, other_owners[:KF - SLOTS]])
    return jax.random.permutation(key_c, listed).astype(jnp.int32)


def draw_owner_lists(key, part):
    key = jax.random.fold_in(key, 11)
    return jax.vmap(owner_row)(jax.random.split(key, N_FSDP))


def symmetric_blocks(key, diagonal_lo, diagonal_hi, spread):
    key_a, key_b = jax.random.split(key)
    full_shape = (N_DP, N_FSDP, SLOTS, BLOCK, BLOCK)
    noise_part = jax.random.normal(key_a, full_shape, jnp.float32) * (spread / math.sqrt(BLOCK))
    noise_part = (noise_part + jnp.swapaxes(noise_part, -1, -2)) * math.sqrt(0.5)
    diagonal = jax.random.uniform(key_b, full_shape[:-1], jnp.float32, diagonal_lo, diagonal_hi)
    return noise_part + diagonal[..., None] * jnp.eye(BLOCK, dtype=jnp.float32)


def draw_left_stats(key, part):
    key = jax.random.fold_in(key, 5)
    return symmetric_blocks(key, 1.0, 8.0, 1.0)


def draw_right_stats(key, part):
    key = jax.random.fold_in(key, 7)
    return symmetric_blocks(key, 1.0, 8.0, 1.0)


def draw_left_roots(key, part):
    key = jax.random.fold_in(key, 13)
    return symmetric_blocks(key, 0.5, 1.5, 0.5).astype(jnp.bfloat16)


def draw_right_roots(key, part):
    key = jax.random.fold_in(key, 17)
    return symmetric_blocks(key, 0.5, 1.5, 0.5).astype(jnp.bfloat16)


def setup_inputs(seed: int = 0) -> dict:
    key_of = jax.random.split(jax.random.key(seed), 7)
    return {
        "gradients": draw_gradients(jax.random.fold_in(key_of[6], 71), 0),
        "owner_lists": draw_owner_lists(jax.random.fold_in(key_of[6], 71), 0),
        "left_stats": draw_left_stats(jax.random.fold_in(key_of[6], 71), 0),
        "right_stats": draw_right_stats(jax.random.fold_in(key_of[6], 71), 0),
        "left_roots": draw_left_roots(jax.random.fold_in(key_of[6], 71), 0),
        "right_roots": draw_right_roots(jax.random.fold_in(key_of[6], 71), 0),
    }


STAT_DECAY = 0.9

def per_block(operands):
    scaled_block, left_pick, right_pick = operands
    gram_left = jnp.dot(scaled_block, scaled_block.T, preferred_element_type=jnp.float32)
    gram_right = jnp.dot(scaled_block.T, scaled_block, preferred_element_type=jnp.float32)
    applied = jnp.dot(left_pick, scaled_block, preferred_element_type=jnp.float32).astype(jnp.bfloat16)
    update = jnp.dot(applied, right_pick, preferred_element_type=jnp.float32).astype(jnp.bfloat16)
    return (gram_left, gram_right, update)

def reference(gradients, owner_lists, left_stats, right_stats, left_roots, right_roots):
    block_total = N_FSDP * KF
    summed = lax.optimization_barrier(jnp.sum(gradients.astype(jnp.float32), axis=0))
    clip_limit = 2.0 * math.sqrt(block_total * BLOCK * BLOCK)
    grad_norm = jnp.sqrt(jnp.sum(summed * summed))
    factor = jnp.minimum(jnp.float32(1.0), clip_limit / (grad_norm + 1e-06))
    scaled = (summed * factor).astype(jnp.bfloat16)
    positions = jnp.arange(KF)
    same_owner = owner_lists[:, :, None] == owner_lists[:, None, :]
    earlier = positions[None, :] < positions[:, None]
    slot_rank = lax.optimization_barrier(jnp.sum(same_owner & earlier[None], axis=2)).reshape(-1).astype(jnp.int32)
    owner_flat = owner_lists.reshape(-1).astype(jnp.int32)
    fsdp_group = (jnp.arange(block_total) // KF).astype(jnp.int32)
    left_pick = left_roots[owner_flat, fsdp_group, slot_rank]
    right_pick = right_roots[owner_flat, fsdp_group, slot_rank]
    gram_left, gram_right, updates = lax.map(per_block, (scaled, left_pick, right_pick))
    mix_new = (1.0 - STAT_DECAY) / BLOCK
    new_left = left_stats.at[owner_flat, fsdp_group, slot_rank].set(STAT_DECAY * left_stats[owner_flat, fsdp_group, slot_rank] + mix_new * gram_left)
    new_right = right_stats.at[owner_flat, fsdp_group, slot_rank].set(STAT_DECAY * right_stats[owner_flat, fsdp_group, slot_rank] + mix_new * gram_right)
    return (new_left, new_right, updates)
```

```python
import functools
import math

import jax
import jax.numpy as jnp
from jax import lax
from jax.experimental import pallas as pl
from jax.experimental.pallas import tpu as pltpu
from jax.sharding import PartitionSpec as P

STAT_DECAY = 0.9
MESH = pl.DeviceIdType.MESH
NZ = 8
NY = 4
NX = 4
HALF = 16
WIDTH = 1024
KF = 8
SLOTS = 6
BF16 = jnp.bfloat16
F32 = jnp.float32


def kernel(
    owner_ref, grad_ref, lstat_ref, rstat_ref, lroot_ref, rroot_ref,
    nleft_ref, nright_ref, upd_ref,
    own_g, got_g, part, lboth, rboth, lpart, rpart, lmine, gall, rall, lhs, lhs2, app,
    norm_z, norm_y, norm_x, norm_c,
    out_s, out_r0, out_r1, out_r2, lst, rst,
    loc_sem, c_ssem, c_rsem, z_ssem, z_rsem, y_ssem, y_rsem, f_ssem, f_rsem,
    n_ssem, n_rsem, o_ssem, o_rsem, fin_sem,
):
    out_r = (out_r0, out_r1, out_r2)
    c = lax.axis_index("dp")
    x = lax.axis_index("fsdp")
    t = lax.axis_index("tensor")
    z, y = t // NY, t % NY
    oc = 1 - c

    def at_z(d):
        return {"tensor": lax.rem(z + d, NZ) * NY + y}

    def at_y(d):
        return {"tensor": z * NY + lax.rem(y + d, NY)}

    def at_x(d):
        return {"fsdp": lax.rem(x + d, NX)}

    at_c = {"dp": oc}

    def remote(src, dst, ssem, rsem, device):
        return pltpu.make_async_remote_copy(
            src_ref=src, dst_ref=dst, send_sem=ssem, recv_sem=rsem,
            device_id=device, device_id_type=MESH,
        )

    local = [
        pltpu.make_async_copy(grad_ref.at[:, c], own_g, loc_sem.at[0]),
        pltpu.make_async_copy(lroot_ref.at[:, c], lboth.at[c], loc_sem.at[1]),
        pltpu.make_async_copy(rroot_ref.at[:, c], rboth.at[c], loc_sem.at[2]),
        pltpu.make_async_copy(lstat_ref, lst, loc_sem.at[3]),
        pltpu.make_async_copy(rstat_ref, rst, loc_sem.at[4]),
    ]
    for copy in local:
        copy.start()

    peers = (
        [at_z(d) for d in range(1, NZ)]
        + [at_y(d) for d in range(1, NY)]
        + [at_x(d) for d in range(1, NX)]
        + [at_c]
    )
    barrier = pltpu.get_barrier_semaphore()
    for peer in peers:
        pl.semaphore_signal(barrier, inc=1, device_id=peer, device_id_type=MESH)
    pl.semaphore_wait(barrier, len(peers))

    halves = [
        remote(grad_ref.at[:, oc], got_g, c_ssem.at[0], c_rsem.at[0], at_c),
        remote(lroot_ref.at[:, oc], lboth.at[c], c_ssem.at[1], c_rsem.at[1], at_c),
        remote(rroot_ref.at[:, oc], rboth.at[c], c_ssem.at[2], c_rsem.at[2], at_c),
    ]
    for copy in halves:
        copy.start()

    owners = [owner_ref[j] for j in range(KF)]
    ranks = []
    for j in range(KF):
        rank = jnp.int32(0)
        for i in range(j):
            rank += jnp.where(owners[i] == owners[j], 1, 0).astype(jnp.int32)
        ranks.append(jnp.minimum(rank, SLOTS - 1))

    local[0].wait()
    halves[0].wait_recv()
    squares = jnp.zeros((HALF, WIDTH), F32)
    for j in range(KF):
        total = own_g[j].astype(F32) + got_g[j].astype(F32)
        part[j] = total.astype(BF16)
        squares += total * total

    def z_sends(k, src, dst):
        return [
            remote(
                src.at[lax.rem(z + d, NZ)], dst, z_ssem.at[k, d], z_rsem.at[k, d], at_z(d)
            )
            for d in range(1, NZ)
        ]

    g_z = z_sends(0, part, gall.at[z, y, c])
    for copy in g_z:
        copy.start()
    gall[z, y, c] = part[z]

    norm_z[z] = jnp.full((8, 128), jnp.sum(squares), F32)
    n_z = [
        remote(norm_z.at[z], norm_z.at[z], n_ssem.at[0, d], n_rsem.at[0, d], at_z(d))
        for d in range(1, NZ)
    ]
    for copy in n_z:
        copy.start()

    local[1].wait()
    halves[1].wait_recv()
    for j in range(KF):
        lpart[j] = lboth[owners[j], ranks[j]]
    local[2].wait()
    halves[2].wait_recv()
    for j in range(KF):
        rpart[j] = rboth[owners[j], ranks[j]]
    lmine[z] = lpart[z]
    rall[z, y, c] = rpart[z]

    row = lax.broadcasted_iota(jnp.int32, (128, WIDTH), 0)
    col = lax.broadcasted_iota(jnp.int32, (128, WIDTH), 1)
    pick = (row // HALF) * 128 + y * 32 + c * HALF + row % HALF
    lhs[pl.ds(128, 128), :] = jnp.where(col == pick, 1.0, 0.0).astype(BF16)

    for copy in n_z:
        copy.wait_recv()
    norm_y[y] = jnp.sum(norm_z[...], axis=0)
    n_y = [
        remote(norm_y.at[y], norm_y.at[y], n_ssem.at[1, d], n_rsem.at[1, d], at_y(d))
        for d in range(1, NY)
    ]
    for copy in n_y:
        copy.start()

    for copy in g_z:
        copy.wait_recv()

    def y_sends(k, buf):
        own = buf.at[:, y, c]
        return [
            remote(own, own, y_ssem.at[k, d], y_rsem.at[k, d], at_y(d)) for d in range(1, NY)
        ]

    def forwards(k, buf):
        return [
            remote(
                buf.at[:, lax.rem(y + NY - d, NY), c], buf.at[:, lax.rem(y + NY - d, NY), c],
                f_ssem.at[k, d], f_rsem.at[k, d], at_c,
            )
            for d in range(NY)
        ]

    g_y = y_sends(0, gall)
    for copy in g_y:
        copy.start()
    g_f = forwards(0, gall)
    g_f[0].start()

    l_z = z_sends(1, lpart, lmine.at[z])
    r_z = z_sends(2, rpart, rall.at[z, y, c])
    for copy in l_z + r_z:
        copy.start()

    for copy in n_y:
        copy.wait_recv()
    norm_x[x] = jnp.sum(norm_y[...], axis=0)
    n_x = [
        remote(norm_x.at[x], norm_x.at[x], n_ssem.at[2, d], n_rsem.at[2, d], at_x(d))
        for d in range(1, NX)
    ]
    for copy in n_x:
        copy.start()
    for copy in n_x:
        copy.wait_recv()
    norm_c[c] = jnp.sum(norm_x[...], axis=0)
    n_c = remote(norm_c.at[c], norm_c.at[c], n_ssem.at[3, 0], n_rsem.at[3, 0], at_c)
    n_c.start()
    n_c.wait_recv()
    clip = 2.0 * math.sqrt(NX * KF * WIDTH * WIDTH)
    norm = jnp.sqrt(norm_c[0] + norm_c[1])
    factor = jnp.minimum(jnp.float32(1.0), clip / (norm + 1e-06))[0:1, 0:1]

    for d in (1, 3, 2):
        g_y[d - 1].wait_recv()
        g_f[d].start()

    for copy in l_z + r_z:
        copy.wait_recv()
    r_y = y_sends(1, rall)
    for copy in r_y:
        copy.start()
    r_f = forwards(1, rall)
    r_f[0].start()

    for copy in g_f:
        copy.wait()
    for copy in g_y:
        copy.wait_send()

    for i in range(NZ):
        gall[i] = (gall[i].astype(F32) * factor).astype(BF16)

    lhs[pl.ds(0, 128), :] = gall[:, y, c].reshape(128, WIDTH)
    lhs2[pl.ds(128, 128), :] = lmine[...].reshape(128, WIDTH)

    def o_sends(k):
        return [
            remote(
                out_s.at[k, lax.rem(z + d, NZ)], out_r[k].at[z, c],
                z_ssem.at[3 + k, d], z_rsem.at[3 + k, d], at_z(d),
            )
            for d in range(1, NZ)
        ]

    nt = (((1,), (1,)), ((), ()))
    for n in range(4):
        g_rows = gall[pl.ds(2 * n, 2)].reshape(256, WIDTH)
        both = lax.dot_general(lhs[...], g_rows, nt, preferred_element_type=F32).astype(BF16)
        out_s[0, :, :, pl.ds(256 * n, 256)] = both[:128].reshape(NZ, HALF, 256)
        lhs2[pl.ds(0, 128), pl.ds(256 * n, 256)] = both[128:]
    o_left = o_sends(0)
    for copy in o_left:
        copy.start()
    for n in range(4):
        g_cols = gall[:, :, :, :, pl.ds(256 * n, 256)].reshape(WIDTH, 256)
        both = jnp.dot(lhs2[...], g_cols, preferred_element_type=F32).astype(BF16)
        out_s[1, :, :, pl.ds(256 * n, 256)] = both[:128].reshape(NZ, HALF, 256)
        app[:, pl.ds(256 * n, 256)] = both[128:]
    o_right = o_sends(1)
    for copy in o_right:
        copy.start()

    for d in (1, 3, 2):
        r_y[d - 1].wait_recv()
        r_f[d].start()
    for copy in r_f:
        copy.wait()
    for copy in r_y:
        copy.wait_send()
    for n in range(4):
        r_cols = rall[:, :, :, :, pl.ds(256 * n, 256)].reshape(WIDTH, 256)
        upd = jnp.dot(app[...], r_cols, preferred_element_type=F32).astype(BF16)
        out_s[2, :, :, pl.ds(256 * n, 256)] = upd.reshape(NZ, HALF, 256)
    o_upd = o_sends(2)
    for copy in o_upd:
        copy.start()
    for k in range(3):
        out_r[k][z, c] = out_s[k, z]

    def finish(k, sends):
        shared = []
        for d in range(NZ):
            if d:
                sends[d - 1].wait_recv()
            here = out_r[k].at[lax.rem(z + NZ - d, NZ), c]
            copy = remote(here, here, o_ssem.at[k, d], o_rsem.at[k, d], at_c)
            copy.start()
            shared.append(copy)
        for copy in shared:
            copy.wait()
        for copy in sends:
            copy.wait_send()

    places, taken = [], []
    for s in range(SLOTS):
        place, count = jnp.int32(0), jnp.int32(0)
        for j in range(KF):
            hit = (owners[j] == c) & (ranks[j] == s)
            place = jnp.where(hit, j, place)
            count = jnp.where(hit, 1, count)
        places.append(place)
        taken.append(count)

    mix = (1.0 - STAT_DECAY) / WIDTH

    def stats(k, buf, out_ref):
        for s in range(SLOTS):
            gram = out_r[k][places[s]].astype(F32)
            new = STAT_DECAY * buf[s] + mix * gram
            buf[s] = jnp.where(taken[s] > 0, new, buf[s])
        copy = pltpu.make_async_copy(buf, out_ref, fin_sem.at[k])
        copy.start()
        return copy

    local[3].wait()
    finish(0, o_left)
    done_left = stats(0, lst, nleft_ref)
    local[4].wait()
    finish(1, o_right)
    done_right = stats(1, rst, nright_ref)
    finish(2, o_upd)
    done_upd = pltpu.make_async_copy(out_r2, upd_ref, fin_sem.at[2])
    done_upd.start()

    for copy in halves + g_z + l_z + r_z + n_z + n_y + n_x + [n_c]:
        copy.wait_send()
    for copy in (done_left, done_right, done_upd):
        copy.wait()


def on_device(gradients, owner_lists, left_stats, right_stats, left_roots, right_roots):
    any_space = pl.BlockSpec(memory_space=pl.ANY)
    vmem, dma = pltpu.VMEM, pltpu.SemaphoreType.DMA
    stat_shape = (SLOTS, 2, HALF, WIDTH)
    new_left, new_right, updates = pl.pallas_call(
        kernel,
        out_shape=[
            jax.ShapeDtypeStruct(stat_shape, F32),
            jax.ShapeDtypeStruct(stat_shape, F32),
            jax.ShapeDtypeStruct((KF, 2, HALF, WIDTH), BF16),
        ],
        in_specs=[pl.BlockSpec(memory_space=pltpu.SMEM)] + [any_space] * 5,
        out_specs=[any_space] * 3,
        scratch_shapes=[
            vmem((KF, HALF, WIDTH), BF16),
            vmem((KF, HALF, WIDTH), BF16),
            vmem((KF, HALF, WIDTH), BF16),
            vmem((2, SLOTS, HALF, WIDTH), BF16),
            vmem((2, SLOTS, HALF, WIDTH), BF16),
            vmem((KF, HALF, WIDTH), BF16),
            vmem((KF, HALF, WIDTH), BF16),
            vmem((NZ, HALF, WIDTH), BF16),
            vmem((NZ, NY, 2, HALF, WIDTH), BF16),
            vmem((NZ, NY, 2, HALF, WIDTH), BF16),
            vmem((256, WIDTH), BF16),
            vmem((256, WIDTH), BF16),
            vmem((128, WIDTH), BF16),
            vmem((NZ, 8, 128), F32),
            vmem((NY, 8, 128), F32),
            vmem((NX, 8, 128), F32),
            vmem((2, 8, 128), F32),
            vmem((3, NZ, HALF, WIDTH), BF16),
            vmem((KF, 2, HALF, WIDTH), BF16),
            vmem((KF, 2, HALF, WIDTH), BF16),
            vmem((KF, 2, HALF, WIDTH), BF16),
            vmem(stat_shape, F32),
            vmem(stat_shape, F32),
            dma((5,)),
            dma((3,)), dma((3,)),
            dma((6, NZ)), dma((6, NZ)),
            dma((2, NY)), dma((2, NY)),
            dma((2, NY)), dma((2, NY)),
            dma((4, NZ)), dma((4, NZ)),
            dma((3, NZ)), dma((3, NZ)),
            dma((3,)),
        ],
        compiler_params=pltpu.CompilerParams(
            collective_id=0, has_side_effects=True, vmem_limit_bytes=60 * 2**20
        ),
    )(
        owner_lists[0],
        gradients.reshape(KF, 2, HALF, WIDTH),
        left_stats.reshape(stat_shape),
        right_stats.reshape(stat_shape),
        left_roots.reshape(stat_shape),
        right_roots.reshape(stat_shape),
    )
    full = (1, 1, SLOTS, 2 * HALF, WIDTH)
    return (
        new_left.reshape(full),
        new_right.reshape(full),
        updates.reshape(KF, 2 * HALF, WIDTH),
    )


def solution(mesh):
    placed = (
        P("dp", "fsdp", "tensor", None),
        P("fsdp", None),
        P("dp", "fsdp", None, "tensor", None),
        P("dp", "fsdp", None, "tensor", None),
        P("dp", "fsdp", None, "tensor", None),
        P("dp", "fsdp", None, "tensor", None),
    )
    return jax.shard_map(
        on_device,
        mesh=mesh,
        in_specs=placed,
        out_specs=(
            P("dp", "fsdp", None, "tensor", None),
            P("dp", "fsdp", None, "tensor", None),
            P("fsdp", "tensor", None),
        ),
        check_vma=False,
    )
```

```python
import functools
import math

import jax
import jax.numpy as jnp
from jax import lax
from jax.experimental import pallas as pl
from jax.experimental.pallas import tpu as pltpu
from jax.sharding import PartitionSpec as P

STAT_DECAY = 0.9
MESH = pl.DeviceIdType.MESH
NZ = 8
NY = 4
NX = 4
HALF = 16
WIDTH = 1024
KF = 8
SLOTS = 6
ORDER = (0, 1, 7, 2, 6, 3, 5, 4)
BATCHES = ((0, 1), (1, 4), (5, 3))
BF16 = jnp.bfloat16
F32 = jnp.float32


def kernel(
    owner_hbm, grad_ref, lstat_ref, rstat_ref, lroot_ref, rroot_ref,
    nleft_ref, nright_ref, upd_ref,
    owner_ref, own_g, got_g, part, lboth, rboth, lpart, rpart, lmine,
    gall, rall, scaled, lhs, lhs2, app, appk,
    norm_y, norm_x, norm_c, norm_z, norm_w,
    out_s, out_r0, out_r1, out_r2, lst, rst,
    loc_sem, c_rsem, z_rsem, gy_rsem, ry_rsem, gf_rsem, rf_rsem, n_rsem, o_rsem, fin_sem, s_sem,
):
    out_r = (out_r0, out_r1, out_r2)
    c = lax.axis_index("dp")
    x = lax.axis_index("fsdp")
    t = lax.axis_index("tensor")
    z, y = t // NY, t % NY
    oc = 1 - c

    def at_z(d):
        return {"tensor": lax.rem(z + d, NZ) * NY + y}

    def at_y(d):
        return {"tensor": z * NY + lax.rem(y + d, NY)}

    def at_x(d):
        return {"fsdp": lax.rem(x + d, NX)}

    def at_c(d):
        return {"dp": oc}

    def remote(src, dst, ssem, rsem, device):
        return pltpu.make_async_remote_copy(
            src_ref=src, dst_ref=dst, send_sem=s_sem.at[ssem], recv_sem=rsem,
            device_id=device, device_id_type=MESH,
        )

    def arrived(ref, rsem):
        remote(ref, ref, 0, rsem, at_c(1)).wait_recv()

    def departed(ref, ssem):
        remote(ref, ref, ssem, fin_sem.at[0], at_c(1)).wait_send()

    local = [
        pltpu.make_async_copy(grad_ref.at[:, c], own_g, loc_sem.at[0]),
        pltpu.make_async_copy(rroot_ref.at[:, c], rboth.at[c], loc_sem.at[1]),
        pltpu.make_async_copy(lroot_ref.at[:, c], lboth.at[c], loc_sem.at[2]),
        pltpu.make_async_copy(owner_hbm, owner_ref, loc_sem.at[3]),
        pltpu.make_async_copy(lstat_ref, lst, loc_sem.at[4]),
        pltpu.make_async_copy(rstat_ref, rst, loc_sem.at[5]),
    ]
    for copy in local[:4]:
        copy.start()

    peers = (
        [at_z(d) for d in range(1, NZ)]
        + [at_y(d) for d in range(1, NY)]
        + [at_x(d) for d in range(1, NX)]
        + [at_c(1)]
    )
    barrier = pltpu.get_barrier_semaphore()
    for peer in peers:
        pl.semaphore_signal(barrier, inc=1, device_id=peer, device_id_type=MESH)
    pl.semaphore_wait(barrier, len(peers))

    remote(grad_ref.at[:, oc], got_g, 0, c_rsem.at[0], at_c(1)).start()
    remote(rroot_ref.at[:, oc], rboth.at[c], 0, c_rsem.at[1], at_c(1)).start()
    remote(lroot_ref.at[:, oc], lboth.at[c], 0, c_rsem.at[2], at_c(1)).start()

    local[0].wait()
    arrived(got_g, c_rsem.at[0])

    def z_send(d, src, dst, rsem):
        remote(src.at[lax.rem(z + d, NZ)], dst, 1, rsem, at_z(d)).start()

    def y_send(d, ref, rsem):
        remote(ref, ref, 2, rsem, at_y(d)).start()

    def share(ref, rsem):
        remote(ref, ref, 3, rsem, at_c(1)).start()

    def batch(b):
        return pl.ds(*BATCHES[b])

    def from_y(d):
        return lax.rem(y + NY - d, NY)

    def pass_on(b):
        own = gall.at[batch(b), y, c]
        for d in (1, 3):
            y_send(d, own, gy_rsem.at[b, d])
        share(own, gf_rsem.at[0])

    squares = jnp.zeros((HALF, WIDTH), F32)
    for k, d in enumerate(ORDER):
        j = lax.rem(z + d, NZ)
        total = own_g[j].astype(F32) + got_g[j].astype(F32)
        squares += total * total
        if d:
            part[j] = total.astype(BF16)
            z_send(d, part, gall.at[k, y, c], z_rsem.at[0 if k < BATCHES[2][0] else 1])
        else:
            gall[0, y, c] = total.astype(BF16)
            pass_on(0)

    def norm_sends(k, buf, here, at, count):
        for d in range(1, count):
            remote(buf.at[here], buf.at[here], 4, n_rsem.at[k], at(d)).start()

    def norm_total(k, buf, count):
        arrived(buf.at[pl.ds(0, count - 1)], n_rsem.at[k])
        return jnp.sum(buf[...], axis=0)

    norm_y[y] = jnp.full((8, 128), jnp.sum(squares), F32)
    norm_sends(0, norm_y, y, at_y, NY)
    for copy in local[4:]:
        copy.start()

    local[3].wait()
    owners = [owner_ref[0, j] for j in range(KF)]
    ranks = []
    for j in range(KF):
        rank = jnp.int32(0)
        for i in range(j):
            rank += jnp.where(owners[i] == owners[j], 1, 0).astype(jnp.int32)
        ranks.append(jnp.minimum(rank, SLOTS - 1))

    local[1].wait()
    arrived(rboth.at[c], c_rsem.at[1])
    for j in range(KF):
        rpart[j] = rboth[owners[j], ranks[j]]
    local[2].wait()
    arrived(lboth.at[c], c_rsem.at[2])
    for j in range(KF):
        lpart[j] = lboth[owners[j], ranks[j]]
    rall[0, y, c] = rpart[z]
    lmine[z] = lpart[z]

    norm_x[x] = norm_total(0, norm_y, NY)
    norm_sends(1, norm_x, x, at_x, NX)

    row = lax.broadcasted_iota(jnp.int32, (128, WIDTH), 0)
    col = lax.broadcasted_iota(jnp.int32, (128, WIDTH), 1)
    pick = (row // HALF) * 128 + y * 32 + c * HALF + row % HALF
    lhs[pl.ds(128, 128), :] = jnp.where(col == pick, 1.0, 0.0).astype(BF16)

    def neighbours(b):
        for d in (1, 3):
            here = gall.at[batch(b), from_y(d), c]
            arrived(here, gy_rsem.at[b, d])
            if d == (1, 3)[b % 2]:
                y_send(d, here, gy_rsem.at[b, 2])
            share(here, gf_rsem.at[d])

    norm_c[c] = norm_total(1, norm_x, NX)
    norm_sends(2, norm_c, c, at_c, 2)
    norm_z[z] = norm_total(2, norm_c, 2)
    norm_sends(3, norm_z, z, at_z, NZ)
    neighbours(0)

    arrived(gall.at[batch(1), y, c], z_rsem.at[0])
    pass_on(1)
    arrived(gall.at[batch(2), y, c], z_rsem.at[1])
    pass_on(2)
    for k, d in enumerate(ORDER):
        if d:
            z_send(d, rpart, rall.at[k, y, c], z_rsem.at[2])
    for d in ORDER[1:]:
        z_send(d, lpart, lmine.at[z], z_rsem.at[3])

    clip = 2.0 * math.sqrt(NX * KF * WIDTH * WIDTH)
    norm = jnp.sqrt(norm_total(3, norm_z, NZ))
    factor = jnp.minimum(jnp.float32(1.0), clip / (norm + 1e-06))[0:1, 0:1]

    def scale(b, yy, cc):
        first, count = BATCHES[b]
        for k in range(first, first + count):
            zz = lax.rem(z + NZ - ORDER[k], NZ)
            scaled[zz, yy, cc] = (gall[k, yy, cc].astype(F32) * factor).astype(BF16)

    for b in range(3):
        scale(b, y, c)
    for d in (1, 3):
        scale(0, from_y(d), c)
    for b in (1, 2):
        neighbours(b)
        for d in (1, 3):
            scale(b, from_y(d), c)

    arrived(rall.at[pl.ds(1, NZ - 1), y, c], z_rsem.at[2])
    own = rall.at[:, y, c]
    for d in (1, 3, 2):
        y_send(d, own, ry_rsem.at[d])
    share(own, rf_rsem.at[0])

    for b in range(3):
        here = gall.at[batch(b), from_y(2), c]
        arrived(here, gy_rsem.at[b, 2])
        share(here, gf_rsem.at[2])
        scale(b, from_y(2), c)
    for d in (0, 1, 3, 2):
        arrived(gall.at[:, from_y(d), oc], gf_rsem.at[d])
        for b in range(3):
            scale(b, from_y(d), oc)
    lhs[pl.ds(0, 128), :] = scaled[:, y, c].reshape(128, WIDTH)

    def o_sends(k):
        for d in ORDER[1:]:
            z_send(d, out_s.at[k], out_r[k].at[z, c], z_rsem.at[4 + k])
        out_r[k][z, c] = out_s[k, z]

    nt = (((1,), (1,)), ((), ()))
    for n in range(4):
        g_rows = scaled[pl.ds(2 * n, 2)].reshape(256, WIDTH)
        both = lax.dot_general(lhs[...], g_rows, nt, preferred_element_type=F32).astype(BF16)
        out_s[0, :, :, pl.ds(256 * n, 256)] = both[:128].reshape(NZ, HALF, 256)
        lhs2[pl.ds(0, 128), pl.ds(256 * n, 256)] = both[128:]
    o_sends(0)
    arrived(lmine.at[pl.ds(0, NZ - 1)], z_rsem.at[3])
    lhs2[pl.ds(128, 128), :] = lmine[...].reshape(128, WIDTH)
    for n in range(4):
        g_cols = scaled[:, :, :, :, pl.ds(256 * n, 256)].reshape(WIDTH, 256)
        both = jnp.dot(lhs2[...], g_cols, preferred_element_type=F32).astype(BF16)
        out_s[1, :, :, pl.ds(256 * n, 256)] = both[:128].reshape(NZ, HALF, 256)
        app[:, pl.ds(256 * n, 256)] = both[128:]
    o_sends(1)

    for k, d in enumerate(ORDER):
        from_z = pl.multiple_of(lax.rem(z + NZ - d, NZ) * 128, 128)
        appk[:, pl.ds(128 * k, 128)] = app[:, pl.ds(from_z, 128)]
    for d in (1, 3, 2):
        here = rall.at[:, from_y(d), c]
        arrived(here, ry_rsem.at[d])
        share(here, rf_rsem.at[0])
    arrived(rall.at[:, :, oc], rf_rsem.at[0])
    for n in range(4):
        r_cols = rall[:, :, :, :, pl.ds(256 * n, 256)].reshape(WIDTH, 256)
        upd = jnp.dot(appk[...], r_cols, preferred_element_type=F32).astype(BF16)
        out_s[2, :, :, pl.ds(256 * n, 256)] = upd.reshape(NZ, HALF, 256)
    o_sends(2)

    places, taken = [], []
    for s in range(SLOTS):
        place, count = jnp.int32(0), jnp.int32(0)
        for j in range(KF):
            hit = (owners[j] == c) & (ranks[j] == s)
            place = jnp.where(hit, j, place)
            count = jnp.where(hit, 1, count)
        places.append(place)
        taken.append(count)

    mix = (1.0 - STAT_DECAY) / WIDTH

    def finish(k):
        arrived(out_r[k].at[pl.ds(0, NZ - 1), c], z_rsem.at[4 + k])
        here = out_r[k].at[:, c]
        remote(here, here, 5, o_rsem.at[k], at_c(1)).start()
        arrived(out_r[k].at[:, oc], o_rsem.at[k])

    def stats(k, buf, out_ref):
        for s in range(SLOTS):
            gram = out_r[k][places[s]].astype(F32)
            new = STAT_DECAY * buf[s] + mix * gram
            buf[s] = jnp.where(taken[s] > 0, new, buf[s])
        copy = pltpu.make_async_copy(buf, out_ref, fin_sem.at[k])
        copy.start()
        return copy

    local[4].wait()
    finish(0)
    done_left = stats(0, lst, nleft_ref)
    local[5].wait()
    finish(1)
    done_right = stats(1, rst, nright_ref)
    finish(2)
    done_upd = pltpu.make_async_copy(out_r2, upd_ref, fin_sem.at[2])
    done_upd.start()

    departed(gall.at[pl.ds(0, 5), :, 0], 0)
    departed(gall.at[pl.ds(0, 7), pl.ds(0, 3)], 1)
    departed(gall.at[pl.ds(0, 6)], 2)
    departed(gall, 3)
    departed(norm_w, 4)
    departed(gall.at[pl.ds(0, 3)], 5)
    for copy in (done_left, done_right, done_upd):
        copy.wait()


def on_device(gradients, owner_lists, left_stats, right_stats, left_roots, right_roots):
    any_space = pl.BlockSpec(memory_space=pl.ANY)
    vmem, dma = pltpu.VMEM, pltpu.SemaphoreType.DMA
    stat_shape = (SLOTS, 2, HALF, WIDTH)
    new_left, new_right, updates = pl.pallas_call(
        kernel,
        out_shape=[
            jax.ShapeDtypeStruct(stat_shape, F32),
            jax.ShapeDtypeStruct(stat_shape, F32),
            jax.ShapeDtypeStruct((KF, 2, HALF, WIDTH), BF16),
        ],
        in_specs=[any_space] * 6,
        out_specs=[any_space] * 3,
        scratch_shapes=[
            pltpu.SMEM((1, KF), jnp.int32),
            vmem((KF, HALF, WIDTH), BF16),
            vmem((KF, HALF, WIDTH), BF16),
            vmem((KF, HALF, WIDTH), BF16),
            vmem((2, SLOTS, HALF, WIDTH), BF16),
            vmem((2, SLOTS, HALF, WIDTH), BF16),
            vmem((KF, HALF, WIDTH), BF16),
            vmem((KF, HALF, WIDTH), BF16),
            vmem((NZ, HALF, WIDTH), BF16),
            vmem((NZ, NY, 2, HALF, WIDTH), BF16),
            vmem((NZ, NY, 2, HALF, WIDTH), BF16),
            vmem((NZ, NY, 2, HALF, WIDTH), BF16),
            vmem((256, WIDTH), BF16),
            vmem((256, WIDTH), BF16),
            vmem((128, WIDTH), BF16),
            vmem((128, WIDTH), BF16),
            vmem((NY, 8, 128), F32),
            vmem((NX, 8, 128), F32),
            vmem((2, 8, 128), F32),
            vmem((NZ, 8, 128), F32),
            vmem((14, 8, 128), F32),
            vmem((3, NZ, HALF, WIDTH), BF16),
            vmem((KF, 2, HALF, WIDTH), BF16),
            vmem((KF, 2, HALF, WIDTH), BF16),
            vmem((KF, 2, HALF, WIDTH), BF16),
            vmem(stat_shape, F32),
            vmem(stat_shape, F32),
            dma((6,)),
            dma((3,)),
            dma((7,)),
            dma((3, NY)),
            dma((NY,)),
            dma((NY,)),
            dma((1,)),
            dma((4,)),
            dma((3,)),
            dma((3,)),
            dma((6,)),
        ],
        compiler_params=pltpu.CompilerParams(
            collective_id=0, has_side_effects=True, vmem_limit_bytes=60 * 2**20
        ),
    )(
        owner_lists,
        gradients.reshape(KF, 2, HALF, WIDTH),
        left_stats.reshape(stat_shape),
        right_stats.reshape(stat_shape),
        left_roots.reshape(stat_shape),
        right_roots.reshape(stat_shape),
    )
    full = (1, 1, SLOTS, 2 * HALF, WIDTH)
    return (
        new_left.reshape(full),
        new_right.reshape(full),
        updates.reshape(KF, 2 * HALF, WIDTH),
    )


def solution(mesh):
    placed = (
        P("dp", "fsdp", "tensor", None),
        P("fsdp", None),
        P("dp", "fsdp", None, "tensor", None),
        P("dp", "fsdp", None, "tensor", None),
        P("dp", "fsdp", None, "tensor", None),
        P("dp", "fsdp", None, "tensor", None),
    )
    return jax.shard_map(
        on_device,
        mesh=mesh,
        in_specs=placed,
        out_specs=(
            P("dp", "fsdp", None, "tensor", None),
            P("dp", "fsdp", None, "tensor", None),
            P("fsdp", "tensor", None),
        ),
        check_vma=False,
    )
```

```python
import functools
import math

import jax
import jax.numpy as jnp
from jax import lax
from jax.experimental import pallas as pl
from jax.experimental.pallas import tpu as pltpu
from jax.sharding import PartitionSpec as P

STAT_DECAY = 0.9
MESH = pl.DeviceIdType.MESH
NZ = 8
NY = 4
NX = 4
HALF = 16
WIDTH = 1024
LANES = 128
WEDGE = 5
KF = 8
SLOTS = 6
ORDER = (0, 1, 7, 2, 6, 3, 5, 4)
BATCHES = ((0, 1), (1, 2), (3, 2), (5, 2), (7, 1))
BF16 = jnp.bfloat16
F32 = jnp.float32


def kernel(
    owner_hbm, grad_ref, lstat_ref, rstat_ref, lroot_ref, rroot_ref,
    nleft_ref, nright_ref, upd_ref,
    owner_ref, own_g, got_g, part, lboth, rboth, lpart, rpart, lmine,
    gall, rh, scaled, rfull, lhs, lhs2, app,
    norm_y, norm_x, norm_c, norm_z, norm_w,
    out_s, out_r0, out_r1, out_r2, lst, rst,
    loc_sem, c_rsem, z_rsem, gy_rsem, ry_rsem, gf_rsem, rf_rsem, n_rsem, o_rsem, fin_sem, s_sem,
):
    out_r = (out_r0, out_r1, out_r2)
    c = lax.axis_index("dp")
    x = lax.axis_index("fsdp")
    t = lax.axis_index("tensor")
    z, y = t // NY, t % NY
    oc = 1 - c

    def at_z(d):
        return {"tensor": lax.rem(z + d, NZ) * NY + y}

    def at_y(d):
        return {"tensor": z * NY + lax.rem(y + d, NY)}

    def at_x(d):
        return {"fsdp": lax.rem(x + d, NX)}

    def at_c(d):
        return {"dp": oc}

    def remote(src, dst, ssem, rsem, device):
        return pltpu.make_async_remote_copy(
            src_ref=src, dst_ref=dst, send_sem=s_sem.at[ssem], recv_sem=rsem,
            device_id=device, device_id_type=MESH,
        )

    def arrived(ref, rsem):
        remote(ref, ref, 0, rsem, at_c(1)).wait_recv()

    def departed(ref, ssem):
        remote(ref, ref, ssem, fin_sem.at[0], at_c(1)).wait_send()

    local = [
        pltpu.make_async_copy(grad_ref.at[:, c], own_g, loc_sem.at[0]),
        pltpu.make_async_copy(rroot_ref.at[:, c], rboth.at[c], loc_sem.at[1]),
        pltpu.make_async_copy(lroot_ref.at[:, c], lboth.at[c], loc_sem.at[2]),
        pltpu.make_async_copy(owner_hbm, owner_ref, loc_sem.at[3]),
        pltpu.make_async_copy(lstat_ref, lst, loc_sem.at[4]),
        pltpu.make_async_copy(rstat_ref, rst, loc_sem.at[5]),
    ]
    for copy in local[:4]:
        copy.start()

    peers = (
        [at_z(d) for d in range(1, NZ)]
        + [at_y(d) for d in range(1, NY)]
        + [at_x(d) for d in range(1, NX)]
        + [at_c(1)]
    )
    barrier = pltpu.get_barrier_semaphore()
    for peer in peers:
        pl.semaphore_signal(barrier, inc=1, device_id=peer, device_id_type=MESH)
    pl.semaphore_wait(barrier, len(peers))

    remote(grad_ref.at[:, oc], got_g, 0, c_rsem.at[0], at_c(1)).start()
    remote(rroot_ref.at[:, oc], rboth.at[c], 0, c_rsem.at[1], at_c(1)).start()
    remote(lroot_ref.at[:, oc], lboth.at[c], 0, c_rsem.at[2], at_c(1)).start()

    local[0].wait()
    arrived(got_g, c_rsem.at[0])

    def z_send(d, src, dst, rsem, ssem=1):
        remote(src.at[lax.rem(z + d, NZ)], dst, ssem, rsem, at_z(d)).start()

    def y_send(d, ref, rsem, ssem=2):
        remote(ref, ref, ssem, rsem, at_y(d)).start()

    def share(ref, rsem, ssem=3):
        remote(ref, ref, ssem, rsem, at_c(1)).start()

    def batch(b):
        return pl.ds(*BATCHES[b])

    def from_y(d):
        return lax.rem(y + NY - d, NY)

    def pass_on(b):
        own = gall.at[batch(b), y, c]
        for d in (1, 3, 2):
            y_send(d, own, gy_rsem.at[b, d])
        share(own, gf_rsem.at[0])

    def wave(b):
        first, count = BATCHES[b]
        for k in range(first, first + count):
            z_send(ORDER[k], part, gall.at[k, y, c], z_rsem.at[b - 1])

    squares = jnp.zeros((HALF, WIDTH), F32)
    for k, d in enumerate(ORDER):
        j = lax.rem(z + d, NZ)
        total = own_g[j].astype(F32) + got_g[j].astype(F32)
        squares += total * total
        if d:
            part[j] = total.astype(BF16)
        else:
            gall[0, y, c] = total.astype(BF16)
        if k == 2:
            wave(1)
        if k == 4:
            wave(2)

    def norm_sends(k, buf, here, at, count):
        for d in range(1, count):
            remote(buf.at[here], buf.at[here], 4, n_rsem.at[k], at(d)).start()

    def norm_total(k, buf, count):
        arrived(buf.at[pl.ds(0, count - 1)], n_rsem.at[k])
        return jnp.sum(buf[...], axis=0)

    norm_y[y] = jnp.full((8, 128), jnp.sum(squares), F32)
    norm_sends(0, norm_y, y, at_y, NY)
    pass_on(0)
    for copy in local[4:]:
        copy.start()

    local[3].wait()
    owners = [owner_ref[0, j] for j in range(KF)]
    ranks = []
    for j in range(KF):
        rank = jnp.int32(0)
        for i in range(j):
            rank += jnp.where(owners[i] == owners[j], 1, 0).astype(jnp.int32)
        ranks.append(jnp.minimum(rank, SLOTS - 1))

    def wedge(both, parts, half):
        for j in range(KF):
            for m in range(WEDGE):
                there = pl.multiple_of(lax.rem(z + m, NZ) * LANES, LANES)
                parts[j, :, pl.ds(LANES * m, LANES)] = both[
                    owners[j], ranks[j], :, pl.ds(there, LANES)
                ]
        half[0, y, c] = parts[z]

    def wedge_sends(parts, half, rsem):
        for d in ORDER[1:]:
            z_send(d, parts, half.at[NZ - d, y, c], rsem, 6)

    def unfold(half, full):
        for k in range(NZ):
            zz = lax.rem(z + k, NZ)
            here = pl.multiple_of(zz * LANES, LANES)
            for m in range(WEDGE):
                tile = half[k, :, :, :, pl.ds(LANES * m, LANES)]
                ww = lax.rem(z + k + m, NZ)
                there = pl.multiple_of(ww * LANES, LANES)
                full[zz, :, :, :, pl.ds(there, LANES)] = tile
                if m in (1, 2, 3):
                    turned = tile.reshape(LANES, LANES).T
                    full[ww, :, :, :, pl.ds(here, LANES)] = turned.reshape(NY, 2, HALF, LANES)

    local[1].wait()
    arrived(rboth.at[c], c_rsem.at[1])
    wedge(rboth, rpart, rh)
    local[2].wait()
    arrived(lboth.at[c], c_rsem.at[2])
    for j in range(KF):
        lpart[j] = lboth[owners[j], ranks[j]]
    lmine[z] = lpart[z]

    arrived(gall.at[batch(1), y, c], z_rsem.at[0])
    wave(3)
    pass_on(1)
    norm_x[x] = norm_total(0, norm_y, NY)
    norm_sends(1, norm_x, x, at_x, NX)
    arrived(gall.at[batch(2), y, c], z_rsem.at[1])
    wave(4)
    pass_on(2)
    norm_c[c] = norm_total(1, norm_x, NX)
    norm_sends(2, norm_c, c, at_c, 2)
    norm_z[z] = norm_total(2, norm_c, 2)
    norm_sends(3, norm_z, z, at_z, NZ)
    arrived(gall.at[batch(3), y, c], z_rsem.at[2])
    wedge_sends(rpart, rh, z_rsem.at[4])
    pass_on(3)
    arrived(gall.at[batch(4), y, c], z_rsem.at[3])
    pass_on(4)
    for d in ORDER[1:]:
        z_send(d, lpart, lmine.at[z], z_rsem.at[5], 9)

    row = lax.broadcasted_iota(jnp.int32, (128, WIDTH), 0)
    col = lax.broadcasted_iota(jnp.int32, (128, WIDTH), 1)
    pick = (row // HALF) * 128 + y * 32 + c * HALF + row % HALF
    lhs[pl.ds(128, 128), :] = jnp.where(col == pick, 1.0, 0.0).astype(BF16)

    clip = 2.0 * math.sqrt(NX * KF * WIDTH * WIDTH)
    norm = jnp.sqrt(norm_total(3, norm_z, NZ))
    factor = jnp.minimum(jnp.float32(1.0), clip / (norm + 1e-06))[0:1, 0:1]

    def scale(b, yy, cc):
        first, count = BATCHES[b]
        for k in range(first, first + count):
            zz = lax.rem(z + NZ - ORDER[k], NZ)
            scaled[zz, yy, cc] = (gall[k, yy, cc].astype(F32) * factor).astype(BF16)

    for b in range(5):
        scale(b, y, c)
    for b in range(5):
        for d in (1, 3, 2):
            here = gall.at[batch(b), from_y(d), c]
            arrived(here, gy_rsem.at[b, d])
            share(here, gf_rsem.at[d])
        for d in (1, 3, 2):
            scale(b, from_y(d), c)

    def pass_roots(i, half):
        own = half.at[:, y, c]
        arrived(half.at[pl.ds(1, NZ - 1), y, c], z_rsem.at[4 + i])
        for d in (1, 3, 2):
            y_send(d, own, ry_rsem.at[i, d], 7)
        share(own, rf_rsem.at[i], 8)

    def gathered(i, half):
        for d in (1, 3, 2):
            here = half.at[:, from_y(d), c]
            arrived(here, ry_rsem.at[i, d])
            share(here, rf_rsem.at[i], 8)
        arrived(half.at[:, :, oc], rf_rsem.at[i])

    pass_roots(0, rh)

    for d in (0, 1, 3, 2):
        arrived(gall.at[:, from_y(d), oc], gf_rsem.at[d])
        for b in range(5):
            scale(b, from_y(d), oc)
    lhs[pl.ds(0, 128), :] = scaled[:, y, c].reshape(128, WIDTH)

    def o_sends(k):
        for d in ORDER[1:]:
            z_send(d, out_s.at[k], out_r[k].at[z, c], z_rsem.at[6 + k])
        out_r[k][z, c] = out_s[k, z]

    nt = (((1,), (1,)), ((), ()))
    for n in range(4):
        g_rows = scaled[pl.ds(2 * n, 2)].reshape(256, WIDTH)
        both = lax.dot_general(lhs[...], g_rows, nt, preferred_element_type=F32).astype(BF16)
        out_s[0, :, :, pl.ds(256 * n, 256)] = both[:128].reshape(NZ, HALF, 256)
        lhs2[:, pl.ds(256 * n, 256)] = both[128:]
    o_sends(0)
    for n in range(4):
        g_cols = scaled[:, :, :, :, pl.ds(256 * n, 256)].reshape(WIDTH, 256)
        both = jnp.dot(lhs2[...], g_cols, preferred_element_type=F32).astype(BF16)
        out_s[1, :, :, pl.ds(256 * n, 256)] = both.reshape(NZ, HALF, 256)
    o_sends(1)
    gathered(0, rh)
    unfold(rh, rfull)
    arrived(lmine.at[pl.ds(0, NZ - 1)], z_rsem.at[5])
    left = lmine[...].reshape(128, WIDTH)
    for n in range(4):
        g_cols = scaled[:, :, :, :, pl.ds(256 * n, 256)].reshape(WIDTH, 256)
        app[:, pl.ds(256 * n, 256)] = jnp.dot(
            left, g_cols, preferred_element_type=F32
        ).astype(BF16)
    for n in range(4):
        r_cols = rfull[:, :, :, :, pl.ds(256 * n, 256)].reshape(WIDTH, 256)
        upd = jnp.dot(app[...], r_cols, preferred_element_type=F32).astype(BF16)
        out_s[2, :, :, pl.ds(256 * n, 256)] = upd.reshape(NZ, HALF, 256)
    o_sends(2)

    places, taken = [], []
    for s in range(SLOTS):
        place, count = jnp.int32(0), jnp.int32(0)
        for j in range(KF):
            hit = (owners[j] == c) & (ranks[j] == s)
            place = jnp.where(hit, j, place)
            count = jnp.where(hit, 1, count)
        places.append(place)
        taken.append(count)

    mix = (1.0 - STAT_DECAY) / WIDTH

    def finish(k):
        arrived(out_r[k].at[pl.ds(0, NZ - 1), c], z_rsem.at[6 + k])
        here = out_r[k].at[:, c]
        remote(here, here, 5, o_rsem.at[k], at_c(1)).start()
        arrived(out_r[k].at[:, oc], o_rsem.at[k])

    def stats(k, buf, out_ref):
        for s in range(SLOTS):
            gram = out_r[k][places[s]].astype(F32)
            new = STAT_DECAY * buf[s] + mix * gram
            buf[s] = jnp.where(taken[s] > 0, new, buf[s])
        copy = pltpu.make_async_copy(buf, out_ref, fin_sem.at[k])
        copy.start()
        return copy

    local[4].wait()
    finish(0)
    done_left = stats(0, lst, nleft_ref)
    local[5].wait()
    finish(1)
    done_right = stats(1, rst, nright_ref)
    arrived(out_r2.at[pl.ds(0, NZ - 1), c], z_rsem.at[8])
    done_upd = pltpu.make_async_copy(out_r2.at[:, c], upd_ref.at[:, c], fin_sem.at[2])
    done_upd.start()
    remote(out_r2.at[:, c], upd_ref.at[:, c], 5, o_rsem.at[2], at_c(1)).start()
    arrived(upd_ref.at[:, oc], o_rsem.at[2])

    departed(gall.at[pl.ds(0, 5), :, 0], 0)
    departed(gall.at[pl.ds(0, 7), pl.ds(0, 2)], 1)
    departed(lpart.at[pl.ds(0, 7)], 9)
    departed(gall.at[pl.ds(0, 3)], 2)
    departed(gall.at[pl.ds(0, 4)], 3)
    departed(rpart.at[pl.ds(0, 7)], 6)
    departed(rh.at[pl.ds(0, 3)], 7)
    departed(rh.at[pl.ds(0, 4)], 8)
    departed(norm_w, 4)
    departed(gall.at[pl.ds(0, 3)], 5)
    for copy in (done_left, done_right, done_upd):
        copy.wait()


def on_device(gradients, owner_lists, left_stats, right_stats, left_roots, right_roots):
    any_space = pl.BlockSpec(memory_space=pl.ANY)
    vmem, dma = pltpu.VMEM, pltpu.SemaphoreType.DMA
    stat_shape = (SLOTS, 2, HALF, WIDTH)
    new_left, new_right, updates = pl.pallas_call(
        kernel,
        out_shape=[
            jax.ShapeDtypeStruct(stat_shape, F32),
            jax.ShapeDtypeStruct(stat_shape, F32),
            jax.ShapeDtypeStruct((KF, 2, HALF, WIDTH), BF16),
        ],
        in_specs=[any_space] * 6,
        out_specs=[any_space] * 3,
        scratch_shapes=[
            pltpu.SMEM((1, KF), jnp.int32),
            vmem((KF, HALF, WIDTH), BF16),
            vmem((KF, HALF, WIDTH), BF16),
            vmem((KF, HALF, WIDTH), BF16),
            vmem((2, SLOTS, HALF, WIDTH), BF16),
            vmem((2, SLOTS, HALF, WIDTH), BF16),
            vmem((KF, HALF, WIDTH), BF16),
            vmem((KF, HALF, WEDGE * LANES), BF16),
            vmem((NZ, HALF, WIDTH), BF16),
            vmem((NZ, NY, 2, HALF, WIDTH), BF16),
            vmem((NZ, NY, 2, HALF, WEDGE * LANES), BF16),
            vmem((NZ, NY, 2, HALF, WIDTH), BF16),
            vmem((NZ, NY, 2, HALF, WIDTH), BF16),
            vmem((256, WIDTH), BF16),
            vmem((128, WIDTH), BF16),
            vmem((128, WIDTH), BF16),
            vmem((NY, 8, 128), F32),
            vmem((NX, 8, 128), F32),
            vmem((2, 8, 128), F32),
            vmem((NZ, 8, 128), F32),
            vmem((14, 8, 128), F32),
            vmem((3, NZ, HALF, WIDTH), BF16),
            vmem((KF, 2, HALF, WIDTH), BF16),
            vmem((KF, 2, HALF, WIDTH), BF16),
            vmem((KF, 2, HALF, WIDTH), BF16),
            vmem(stat_shape, F32),
            vmem(stat_shape, F32),
            dma((6,)),
            dma((3,)),
            dma((9,)),
            dma((5, NY)),
            dma((1, NY)),
            dma((NY,)),
            dma((1,)),
            dma((4,)),
            dma((3,)),
            dma((3,)),
            dma((10,)),
        ],
        compiler_params=pltpu.CompilerParams(
            collective_id=0, has_side_effects=True, vmem_limit_bytes=60 * 2**20
        ),
    )(
        owner_lists,
        gradients.reshape(KF, 2, HALF, WIDTH),
        left_stats.reshape(stat_shape),
        right_stats.reshape(stat_shape),
        left_roots.reshape(stat_shape),
        right_roots.reshape(stat_shape),
    )
    full = (1, 1, SLOTS, 2 * HALF, WIDTH)
    return (
        new_left.reshape(full),
        new_right.reshape(full),
        updates.reshape(KF, 2 * HALF, WIDTH),
    )


def solution(mesh):
    placed = (
        P("dp", "fsdp", "tensor", None),
        P("fsdp", None),
        P("dp", "fsdp", None, "tensor", None),
        P("dp", "fsdp", None, "tensor", None),
        P("dp", "fsdp", None, "tensor", None),
        P("dp", "fsdp", None, "tensor", None),
    )
    return jax.shard_map(
        on_device,
        mesh=mesh,
        in_specs=placed,
        out_specs=(
            P("dp", "fsdp", None, "tensor", None),
            P("dp", "fsdp", None, "tensor", None),
            P("fsdp", "tensor", None),
        ),
        check_vma=False,
    )
```

```python
import functools
import math

import jax
import jax.numpy as jnp
from jax import lax
from jax.experimental import pallas as pl
from jax.experimental.pallas import tpu as pltpu
from jax.sharding import PartitionSpec as P

STAT_DECAY = 0.9
MESH = pl.DeviceIdType.MESH
NZ = 8
NY = 4
NX = 4
HALF = 16
WIDTH = 1024
LANES = 128
WEDGE = 5
KF = 8
SLOTS = 6
ORDER = (0, 1, 7, 2, 6, 3, 5, 4)
BATCHES = ((0, 1), (1, 2), (3, 2), (5, 2), (7, 1))
BF16 = jnp.bfloat16
F32 = jnp.float32


def kernel(
    owner_hbm, grad_ref, lstat_ref, rstat_ref, lroot_ref, rroot_ref,
    nleft_ref, nright_ref, upd_ref,
    owner_ref, own_g, got_g, part, lboth, rboth, lpart, rpart, lmine,
    gall, rh, scaled, rfull, lhs, lhs2, left, app,
    norm_y, norm_x, norm_c, norm_z, norm_w,
    out_s, out_r0, out_r1, out_r2, lst, rst,
    loc_sem, c_rsem, z_rsem, gy_rsem, ry_rsem, gf_rsem, rf_rsem, n_rsem, o_rsem, fin_sem, s_sem,
):
    out_r = (out_r0, out_r1, out_r2)
    c = lax.axis_index("dp")
    x = lax.axis_index("fsdp")
    t = lax.axis_index("tensor")
    z, y = t // NY, t % NY
    oc = 1 - c

    def at_z(d):
        return {"tensor": lax.rem(z + d, NZ) * NY + y}

    def at_y(d):
        return {"tensor": z * NY + lax.rem(y + d, NY)}

    def at_x(d):
        return {"fsdp": lax.rem(x + d, NX)}

    def at_c(d):
        return {"dp": oc}

    def remote(src, dst, ssem, rsem, device):
        return pltpu.make_async_remote_copy(
            src_ref=src, dst_ref=dst, send_sem=s_sem.at[ssem], recv_sem=rsem,
            device_id=device, device_id_type=MESH,
        )

    def arrived(ref, rsem):
        remote(ref, ref, 0, rsem, at_c(1)).wait_recv()

    def departed(ref, ssem):
        remote(ref, ref, ssem, fin_sem.at[0], at_c(1)).wait_send()

    local = [
        pltpu.make_async_copy(grad_ref.at[:, c], own_g, loc_sem.at[0]),
        pltpu.make_async_copy(rroot_ref.at[:, c], rboth.at[c], loc_sem.at[1]),
        pltpu.make_async_copy(lroot_ref.at[:, c], lboth.at[c], loc_sem.at[2]),
        pltpu.make_async_copy(owner_hbm, owner_ref, loc_sem.at[3]),
        pltpu.make_async_copy(lstat_ref, lst, loc_sem.at[4]),
        pltpu.make_async_copy(rstat_ref, rst, loc_sem.at[5]),
    ]
    for copy in local[:4]:
        copy.start()

    peers = (
        [at_z(d) for d in range(1, NZ)]
        + [at_y(d) for d in range(1, NY)]
        + [at_x(d) for d in range(1, NX)]
        + [at_c(1)]
    )
    barrier = pltpu.get_barrier_semaphore()
    for peer in peers:
        pl.semaphore_signal(barrier, inc=1, device_id=peer, device_id_type=MESH)
    pl.semaphore_wait(barrier, len(peers))

    remote(grad_ref.at[:, oc], got_g, 0, c_rsem.at[0], at_c(1)).start()
    remote(rroot_ref.at[:, oc], rboth.at[c], 0, c_rsem.at[1], at_c(1)).start()
    remote(lroot_ref.at[:, oc], lboth.at[c], 0, c_rsem.at[2], at_c(1)).start()

    local[0].wait()
    arrived(got_g, c_rsem.at[0])

    def z_send(d, src, dst, rsem, ssem=1):
        remote(src.at[lax.rem(z + d, NZ)], dst, ssem, rsem, at_z(d)).start()

    def y_send(d, ref, rsem, ssem=2):
        remote(ref, ref, ssem, rsem, at_y(d)).start()

    def share(ref, rsem, ssem=3):
        remote(ref, ref, ssem, rsem, at_c(1)).start()

    def batch(b):
        return pl.ds(*BATCHES[b])

    def from_y(d):
        return lax.rem(y + NY - d, NY)

    def pass_on(b):
        own = gall.at[batch(b), y, c]
        for d in (1, 3, 2):
            y_send(d, own, gy_rsem.at[b, d])
        share(own, gf_rsem.at[b])

    def wave(b):
        first, count = BATCHES[b]
        for k in range(first, first + count):
            z_send(ORDER[k], part, gall.at[k, y, c], z_rsem.at[b - 1])

    squares = jnp.zeros((HALF, WIDTH), F32)
    for k, d in enumerate(ORDER):
        j = lax.rem(z + d, NZ)
        total = own_g[j].astype(F32) + got_g[j].astype(F32)
        squares += total * total
        if d:
            part[j] = total.astype(BF16)
        else:
            gall[0, y, c] = total.astype(BF16)
        if k == 2:
            wave(1)

    def norm_sends(k, buf, here, at, count):
        for d in range(1, count):
            remote(buf.at[here], buf.at[here], 4, n_rsem.at[k], at(d)).start()

    def norm_total(k, buf, count):
        arrived(buf.at[pl.ds(0, count - 1)], n_rsem.at[k])
        return jnp.sum(buf[...], axis=0)

    norm_y[y] = jnp.full((8, 128), jnp.sum(squares), F32)
    norm_sends(0, norm_y, y, at_y, NY)
    pass_on(0)
    for copy in local[4:]:
        copy.start()

    local[3].wait()
    owners = [owner_ref[0, j] for j in range(KF)]
    ranks = []
    for j in range(KF):
        rank = jnp.int32(0)
        for i in range(j):
            rank += jnp.where(owners[i] == owners[j], 1, 0).astype(jnp.int32)
        ranks.append(jnp.minimum(rank, SLOTS - 1))

    def wedge(both, parts, half):
        for j in range(KF):
            for m in range(WEDGE):
                there = pl.multiple_of(lax.rem(z + m, NZ) * LANES, LANES)
                parts[j, :, pl.ds(LANES * m, LANES)] = both[
                    owners[j], ranks[j], :, pl.ds(there, LANES)
                ]
        half[0, y, c] = parts[z]

    def wedge_sends(parts, half, rsem, order=ORDER[1:]):
        for d in order:
            z_send(d, parts, half.at[NZ - d, y, c], rsem, 6)

    def unfold(half, full):
        for k in range(NZ):
            zz = lax.rem(z + k, NZ)
            here = pl.multiple_of(zz * LANES, LANES)
            for m in range(WEDGE):
                tile = half[k, :, :, :, pl.ds(LANES * m, LANES)]
                ww = lax.rem(z + k + m, NZ)
                there = pl.multiple_of(ww * LANES, LANES)
                full[zz, :, :, :, pl.ds(there, LANES)] = tile
                if m in (1, 2, 3):
                    turned = tile.reshape(LANES, LANES).T
                    full[ww, :, :, :, pl.ds(here, LANES)] = turned.reshape(NY, 2, HALF, LANES)

    local[1].wait()
    arrived(rboth.at[c], c_rsem.at[1])
    wedge(rboth, rpart, rh)
    local[2].wait()
    arrived(lboth.at[c], c_rsem.at[2])
    for j in range(KF):
        lpart[j] = lboth[owners[j], ranks[j]]
    lmine[z] = lpart[z]

    wave(2)
    wave(3)
    arrived(gall.at[batch(1), y, c], z_rsem.at[0])
    pass_on(1)
    norm_x[x] = norm_total(0, norm_y, NY)
    norm_sends(1, norm_x, x, at_x, NX)
    wave(4)
    arrived(gall.at[batch(2), y, c], z_rsem.at[1])
    pass_on(2)
    norm_c[c] = norm_total(1, norm_x, NX)
    norm_sends(2, norm_c, c, at_c, 2)
    norm_z[z] = norm_total(2, norm_c, 2)
    norm_sends(3, norm_z, z, at_z, NZ)
    wedge_sends(rpart, rh, z_rsem.at[4])
    arrived(gall.at[batch(3), y, c], z_rsem.at[2])
    pass_on(3)
    arrived(gall.at[batch(4), y, c], z_rsem.at[3])
    pass_on(4)
    for d in ORDER[1:]:
        z_send(d, lpart, lmine.at[z], z_rsem.at[5], 9)

    row = lax.broadcasted_iota(jnp.int32, (128, WIDTH), 0)
    col = lax.broadcasted_iota(jnp.int32, (128, WIDTH), 1)
    pick = (row // HALF) * 128 + y * 32 + c * HALF + row % HALF
    one_hot = jnp.where(col == pick, 1.0, 0.0).astype(BF16)
    lhs[pl.ds(NZ, NZ)] = one_hot.reshape(NZ, HALF, WIDTH)

    clip = 2.0 * math.sqrt(NX * KF * WIDTH * WIDTH)
    norm = jnp.sqrt(norm_total(3, norm_z, NZ))
    factor = jnp.minimum(jnp.float32(1.0), clip / (norm + 1e-06))[0:1, 0:1]

    def times(ref):
        return (ref[...].astype(F32) * factor).astype(BF16)

    def column(k):
        return pl.multiple_of(lax.rem(z + NZ - ORDER[k], NZ) * LANES, LANES)

    for k in range(NZ):
        lhs[lax.rem(z + NZ - ORDER[k], NZ)] = times(gall.at[k, y, c])

    nt = (((1,), (1,)), ((), ()))

    def whole(b):
        arrived(gall.at[batch(b), :, oc], gf_rsem.at[b])
        first, count = BATCHES[b]
        for k in range(first, first + count):
            scaled[k] = times(gall.at[k])
        if b == 0:
            return
        n = b - 1
        both = lax.dot_general(
            lhs[...].reshape(256, WIDTH), scaled[pl.ds(2 * n, 2)].reshape(256, WIDTH), nt,
            preferred_element_type=F32,
        ).astype(BF16)
        for q in range(2):
            tile = both[:128, LANES * q:LANES * (q + 1)].reshape(NZ, HALF, LANES)
            out_s[0, :, :, pl.ds(column(2 * n + q), LANES)] = tile
        lhs2[:, pl.ds(256 * n, 256)] = both[128:]

    def pass_roots(i, half):
        own = half.at[:, y, c]
        arrived(half.at[pl.ds(1, NZ - 1), y, c], z_rsem.at[4 + i])
        for d in (1, 3, 2):
            y_send(d, own, ry_rsem.at[i, d], 7)
        share(own, rf_rsem.at[i], 8)

    for b in range(5):
        for d in (1, 3, 2):
            here = gall.at[batch(b), from_y(d), c]
            arrived(here, gy_rsem.at[b, d])
            share(here, gf_rsem.at[b])
        if b:
            whole(b - 1)
    pass_roots(0, rh)
    whole(4)

    def gathered(i, half):
        for d in (1, 3, 2):
            here = half.at[:, from_y(d), c]
            arrived(here, ry_rsem.at[i, d])
            share(here, rf_rsem.at[i], 8)
        arrived(half.at[:, :, oc], rf_rsem.at[i])

    def o_sends(k):
        for d in ORDER[1:]:
            z_send(d, out_s.at[k], out_r[k].at[z, c], z_rsem.at[6 + k])
        out_r[k][z, c] = out_s[k, z]

    o_sends(0)
    for n in range(4):
        g_cols = scaled[:, :, :, :, pl.ds(256 * n, 256)].reshape(WIDTH, 256)
        both = jnp.dot(lhs2[...], g_cols, preferred_element_type=F32).astype(BF16)
        out_s[1, :, :, pl.ds(256 * n, 256)] = both.reshape(NZ, HALF, 256)
    o_sends(1)
    arrived(lmine.at[pl.ds(0, NZ - 1)], z_rsem.at[5])
    for k in range(NZ):
        left[:, :, pl.ds(LANES * k, LANES)] = lmine[:, :, pl.ds(column(k), LANES)]
    for n in range(4):
        g_cols = scaled[:, :, :, :, pl.ds(256 * n, 256)].reshape(WIDTH, 256)
        app[:, pl.ds(256 * n, 256)] = jnp.dot(
            left[...].reshape(128, WIDTH), g_cols, preferred_element_type=F32
        ).astype(BF16)
    gathered(0, rh)
    unfold(rh, rfull)
    for n in range(4):
        r_cols = rfull[:, :, :, :, pl.ds(256 * n, 256)].reshape(WIDTH, 256)
        upd = jnp.dot(app[...], r_cols, preferred_element_type=F32).astype(BF16)
        out_s[2, :, :, pl.ds(256 * n, 256)] = upd.reshape(NZ, HALF, 256)
    o_sends(2)

    places, taken = [], []
    for s in range(SLOTS):
        place, count = jnp.int32(0), jnp.int32(0)
        for j in range(KF):
            hit = (owners[j] == c) & (ranks[j] == s)
            place = jnp.where(hit, j, place)
            count = jnp.where(hit, 1, count)
        places.append(place)
        taken.append(count)

    mix = (1.0 - STAT_DECAY) / WIDTH

    def finish(k):
        arrived(out_r[k].at[pl.ds(0, NZ - 1), c], z_rsem.at[6 + k])
        here = out_r[k].at[:, c]
        remote(here, here, 5, o_rsem.at[k], at_c(1)).start()
        arrived(out_r[k].at[:, oc], o_rsem.at[k])

    def stats(k, buf, out_ref):
        for s in range(SLOTS):
            gram = out_r[k][places[s]].astype(F32)
            new = STAT_DECAY * buf[s] + mix * gram
            buf[s] = jnp.where(taken[s] > 0, new, buf[s])
        copy = pltpu.make_async_copy(buf, out_ref, fin_sem.at[k])
        copy.start()
        return copy

    local[4].wait()
    finish(0)
    done_left = stats(0, lst, nleft_ref)
    local[5].wait()
    finish(1)
    done_right = stats(1, rst, nright_ref)
    arrived(out_r2.at[pl.ds(0, NZ - 1), c], z_rsem.at[8])
    done_upd = pltpu.make_async_copy(out_r2.at[:, c], upd_ref.at[:, c], fin_sem.at[2])
    done_upd.start()
    remote(out_r2.at[:, c], upd_ref.at[:, c], 5, o_rsem.at[2], at_c(1)).start()
    arrived(upd_ref.at[:, oc], o_rsem.at[2])

    departed(gall.at[pl.ds(0, 5), :, 0], 0)
    departed(gall.at[pl.ds(0, 7), pl.ds(0, 2)], 1)
    departed(lpart.at[pl.ds(0, 7)], 9)
    departed(gall.at[pl.ds(0, 3)], 2)
    departed(gall.at[pl.ds(0, 4)], 3)
    departed(rpart.at[pl.ds(0, 7)], 6)
    departed(rh.at[pl.ds(0, 3)], 7)
    departed(rh.at[pl.ds(0, 4)], 8)
    departed(norm_w, 4)
    departed(gall.at[pl.ds(0, 3)], 5)
    for copy in (done_left, done_right, done_upd):
        copy.wait()


def hand_over(*refs):
    sems = refs[9]
    pieces = [(i, n) for i in range(3) for n in range(2)]
    halves = [refs[i].shape[0] // 2 for i in range(3)]

    def part(i, n):
        return pl.ds(n * halves[i], halves[i])

    loads = [
        pltpu.make_async_copy(
            refs[i].at[part(i, n)], refs[6 + i].at[part(i, n)], sems.at[0, i, n]
        )
        for i, n in pieces
    ]
    stores = [
        pltpu.make_async_copy(
            refs[6 + i].at[part(i, n)], refs[3 + i].at[part(i, n)], sems.at[1, i, n]
        )
        for i, n in pieces
    ]
    for copy in loads:
        copy.start()
    for load, store in zip(loads, stores):
        load.wait()
        store.start()
    for copy in stores:
        copy.wait()


def on_device(gradients, owner_lists, left_stats, right_stats, left_roots, right_roots):
    any_space = pl.BlockSpec(memory_space=pl.ANY)
    vmem, dma = pltpu.VMEM, pltpu.SemaphoreType.DMA
    stat_shape = (SLOTS, 2, HALF, WIDTH)
    new_left, new_right, updates = pl.pallas_call(
        kernel,
        out_shape=[
            jax.ShapeDtypeStruct(stat_shape, F32),
            jax.ShapeDtypeStruct(stat_shape, F32),
            jax.ShapeDtypeStruct((KF, 2, HALF, WIDTH), BF16),
        ],
        in_specs=[any_space] * 6,
        out_specs=[any_space] * 3,
        scratch_shapes=[
            pltpu.SMEM((1, KF), jnp.int32),
            vmem((KF, HALF, WIDTH), BF16),
            vmem((KF, HALF, WIDTH), BF16),
            vmem((KF, HALF, WIDTH), BF16),
            vmem((2, SLOTS, HALF, WIDTH), BF16),
            vmem((2, SLOTS, HALF, WIDTH), BF16),
            vmem((KF, HALF, WIDTH), BF16),
            vmem((KF, HALF, WEDGE * LANES), BF16),
            vmem((NZ, HALF, WIDTH), BF16),
            vmem((NZ, NY, 2, HALF, WIDTH), BF16),
            vmem((NZ, NY, 2, HALF, WEDGE * LANES), BF16),
            vmem((NZ, NY, 2, HALF, WIDTH), BF16),
            vmem((NZ, NY, 2, HALF, WIDTH), BF16),
            vmem((2 * NZ, HALF, WIDTH), BF16),
            vmem((128, WIDTH), BF16),
            vmem((NZ, HALF, WIDTH), BF16),
            vmem((128, WIDTH), BF16),
            vmem((NY, 8, 128), F32),
            vmem((NX, 8, 128), F32),
            vmem((2, 8, 128), F32),
            vmem((NZ, 8, 128), F32),
            vmem((14, 8, 128), F32),
            vmem((3, NZ, HALF, WIDTH), BF16),
            vmem((KF, 2, HALF, WIDTH), BF16),
            vmem((KF, 2, HALF, WIDTH), BF16),
            vmem((KF, 2, HALF, WIDTH), BF16),
            vmem(stat_shape, F32),
            vmem(stat_shape, F32),
            dma((6,)),
            dma((3,)),
            dma((9,)),
            dma((5, NY)),
            dma((1, NY)),
            dma((5,)),
            dma((1,)),
            dma((4,)),
            dma((3,)),
            dma((3,)),
            dma((10,)),
        ],
        compiler_params=pltpu.CompilerParams(
            collective_id=0, has_side_effects=True, vmem_limit_bytes=60 * 2**20
        ),
    )(
        owner_lists,
        gradients.reshape(KF, 2, HALF, WIDTH),
        left_stats.reshape(stat_shape),
        right_stats.reshape(stat_shape),
        left_roots.reshape(stat_shape),
        right_roots.reshape(stat_shape),
    )
    new_left, new_right, updates = pl.pallas_call(
        hand_over,
        out_shape=[
            jax.ShapeDtypeStruct(stat_shape, F32),
            jax.ShapeDtypeStruct(stat_shape, F32),
            jax.ShapeDtypeStruct((KF, 2, HALF, WIDTH), BF16),
        ],
        in_specs=[any_space] * 3,
        out_specs=[any_space] * 3,
        scratch_shapes=[
            vmem(stat_shape, F32),
            vmem(stat_shape, F32),
            vmem((KF, 2, HALF, WIDTH), BF16),
            dma((2, 3, 2)),
        ],
        compiler_params=pltpu.CompilerParams(vmem_limit_bytes=60 * 2**20),
    )(new_left, new_right, updates)
    full = (1, 1, SLOTS, 2 * HALF, WIDTH)
    return (
        new_left.reshape(full),
        new_right.reshape(full),
        updates.reshape(KF, 2 * HALF, WIDTH),
    )


def solution(mesh):
    placed = (
        P("dp", "fsdp", "tensor", None),
        P("fsdp", None),
        P("dp", "fsdp", None, "tensor", None),
        P("dp", "fsdp", None, "tensor", None),
        P("dp", "fsdp", None, "tensor", None),
        P("dp", "fsdp", None, "tensor", None),
    )
    return jax.shard_map(
        on_device,
        mesh=mesh,
        in_specs=placed,
        out_specs=(
            P("dp", "fsdp", None, "tensor", None),
            P("dp", "fsdp", None, "tensor", None),
            P("fsdp", "tensor", None),
        ),
        check_vma=False,
    )
```

```python
import functools
import math

import jax
import jax.numpy as jnp
from jax import lax
from jax.experimental import pallas as pl
from jax.experimental.pallas import tpu as pltpu
from jax.sharding import PartitionSpec as P

STAT_DECAY = 0.9
MESH = pl.DeviceIdType.MESH
NZ = 8
NY = 4
NX = 4
HALF = 16
WIDTH = 1024
LANES = 128
WEDGE = 5
KF = 8
SLOTS = 6
ORDER = (0, 1, 7, 2, 6, 3, 5, 4)
BATCHES = ((0, 1), (1, 2), (3, 2), (5, 2), (7, 1))
LEFT_RUNS = ((0, 1), (1, 1), (2, 1), (3, 1))
BF16 = jnp.bfloat16
F32 = jnp.float32


def kernel(
    owner_hbm, grad_ref, lstat_ref, rstat_ref, lroot_ref, rroot_ref,
    nleft_ref, nright_ref, upd_ref,
    owner_ref, own_g, got_g, part, lboth, rboth, lpart, rpart, lmine,
    gall, rh, scaled, rfull, lhs, lhs2, left, app,
    norm_y, norm_x, norm_c, norm_z, norm_w,
    left_s, out_s, out_r0, out_r1, out_r2, lst, rst,
    loc_sem, c_rsem, z_rsem, gy_rsem, ry_rsem, gf_rsem, rf_rsem, n_rsem, o_rsem, fin_sem, s_sem,
):
    out_r = (out_r0, out_r1, out_r2)
    c = lax.axis_index("dp")
    x = lax.axis_index("fsdp")
    t = lax.axis_index("tensor")
    z, y = t // NY, t % NY
    oc = 1 - c

    def at_z(d):
        return {"tensor": lax.rem(z + d, NZ) * NY + y}

    def at_y(d):
        return {"tensor": z * NY + lax.rem(y + d, NY)}

    def at_x(d):
        return {"fsdp": lax.rem(x + d, NX)}

    def at_c(d):
        return {"dp": oc}

    def remote(src, dst, ssem, rsem, device):
        return pltpu.make_async_remote_copy(
            src_ref=src, dst_ref=dst, send_sem=s_sem.at[ssem], recv_sem=rsem,
            device_id=device, device_id_type=MESH,
        )

    def arrived(ref, rsem):
        remote(ref, ref, 0, rsem, at_c(1)).wait_recv()

    def departed(ref, ssem):
        remote(ref, ref, ssem, fin_sem.at[0], at_c(1)).wait_send()

    local = [
        pltpu.make_async_copy(grad_ref.at[:, c], own_g, loc_sem.at[0]),
        pltpu.make_async_copy(rroot_ref.at[:, c], rboth.at[c], loc_sem.at[1]),
        pltpu.make_async_copy(lroot_ref.at[:, c], lboth.at[c], loc_sem.at[2]),
        pltpu.make_async_copy(owner_hbm, owner_ref, loc_sem.at[3]),
        pltpu.make_async_copy(lstat_ref, lst, loc_sem.at[4]),
        pltpu.make_async_copy(rstat_ref, rst, loc_sem.at[5]),
    ]
    for copy in local[:4]:
        copy.start()

    peers = (
        [at_z(d) for d in range(1, NZ)]
        + [at_y(d) for d in range(1, NY)]
        + [at_x(d) for d in range(1, NX)]
        + [at_c(1)]
    )
    barrier = pltpu.get_barrier_semaphore()
    for peer in peers:
        pl.semaphore_signal(barrier, inc=1, device_id=peer, device_id_type=MESH)
    pl.semaphore_wait(barrier, len(peers))

    remote(grad_ref.at[:, oc], got_g, 0, c_rsem.at[0], at_c(1)).start()
    remote(rroot_ref.at[:, oc], rboth.at[c], 0, c_rsem.at[1], at_c(1)).start()
    remote(lroot_ref.at[:, oc], lboth.at[c], 0, c_rsem.at[2], at_c(1)).start()

    local[0].wait()
    arrived(got_g, c_rsem.at[0])

    def z_send(d, src, dst, rsem, ssem=1):
        remote(src.at[lax.rem(z + d, NZ)], dst, ssem, rsem, at_z(d)).start()

    def y_send(d, ref, rsem, ssem=2):
        remote(ref, ref, ssem, rsem, at_y(d)).start()

    def share(ref, rsem, ssem=3):
        remote(ref, ref, ssem, rsem, at_c(1)).start()

    def batch(b):
        return pl.ds(*BATCHES[b])

    def from_y(d):
        return lax.rem(y + NY - d, NY)

    def pass_on(b):
        own = gall.at[batch(b), y, c]
        for d in (1, 3, 2):
            y_send(d, own, gy_rsem.at[b, d])
        share(own, gf_rsem.at[b])

    def wave(b):
        first, count = BATCHES[b]
        for k in range(first, first + count):
            z_send(ORDER[k], part, gall.at[k, y, c], z_rsem.at[b - 1])

    squares = jnp.zeros((HALF, WIDTH), F32)
    for k, d in enumerate(ORDER):
        j = lax.rem(z + d, NZ)
        total = own_g[j].astype(F32) + got_g[j].astype(F32)
        squares += total * total
        if d:
            part[j] = total.astype(BF16)
        else:
            gall[0, y, c] = total.astype(BF16)
        if k == 2:
            wave(1)

    def norm_sends(k, buf, here, at, count):
        for d in range(1, count):
            remote(buf.at[here], buf.at[here], 4, n_rsem.at[k], at(d)).start()

    def norm_total(k, buf, count):
        arrived(buf.at[pl.ds(0, count - 1)], n_rsem.at[k])
        return jnp.sum(buf[...], axis=0)

    norm_y[y] = jnp.full((8, 128), jnp.sum(squares), F32)
    norm_sends(0, norm_y, y, at_y, NY)
    pass_on(0)
    for copy in local[4:]:
        copy.start()

    local[3].wait()
    owners = [owner_ref[0, j] for j in range(KF)]
    ranks = []
    for j in range(KF):
        rank = jnp.int32(0)
        for i in range(j):
            rank += jnp.where(owners[i] == owners[j], 1, 0).astype(jnp.int32)
        ranks.append(jnp.minimum(rank, SLOTS - 1))

    def wedge(both, parts, half):
        for j in range(KF):
            for m in range(WEDGE):
                there = pl.multiple_of(lax.rem(z + m, NZ) * LANES, LANES)
                parts[j, :, pl.ds(LANES * m, LANES)] = both[
                    owners[j], ranks[j], :, pl.ds(there, LANES)
                ]
        half[0, y, c] = parts[z]

    def wedge_sends(parts, half, rsem, order=ORDER[1:]):
        for d in order:
            z_send(d, parts, half.at[NZ - d, y, c], rsem, 6)

    def unfold(half, full):
        for k in range(NZ):
            zz = lax.rem(z + k, NZ)
            here = pl.multiple_of(zz * LANES, LANES)
            for m in range(WEDGE):
                tile = half[k, :, :, :, pl.ds(LANES * m, LANES)]
                ww = lax.rem(z + k + m, NZ)
                there = pl.multiple_of(ww * LANES, LANES)
                full[zz, :, :, :, pl.ds(there, LANES)] = tile
                if m in (1, 2, 3):
                    turned = tile.reshape(LANES, LANES).T
                    full[ww, :, :, :, pl.ds(here, LANES)] = turned.reshape(NY, 2, HALF, LANES)

    local[1].wait()
    arrived(rboth.at[c], c_rsem.at[1])
    wedge(rboth, rpart, rh)
    local[2].wait()
    arrived(lboth.at[c], c_rsem.at[2])
    for j in range(KF):
        lpart[j] = lboth[owners[j], ranks[j]]
    lmine[z] = lpart[z]

    wave(2)
    wave(3)
    arrived(gall.at[batch(1), y, c], z_rsem.at[0])
    pass_on(1)
    norm_x[x] = norm_total(0, norm_y, NY)
    norm_sends(1, norm_x, x, at_x, NX)
    wave(4)
    arrived(gall.at[batch(2), y, c], z_rsem.at[1])
    pass_on(2)
    norm_c[c] = norm_total(1, norm_x, NX)
    norm_sends(2, norm_c, c, at_c, 2)
    norm_z[z] = norm_total(2, norm_c, 2)
    norm_sends(3, norm_z, z, at_z, NZ)
    wedge_sends(rpart, rh, z_rsem.at[4])
    arrived(gall.at[batch(3), y, c], z_rsem.at[2])
    pass_on(3)
    arrived(gall.at[batch(4), y, c], z_rsem.at[3])
    pass_on(4)
    for d in ORDER[1:]:
        z_send(d, lpart, lmine.at[z], z_rsem.at[5], 9)

    row = lax.broadcasted_iota(jnp.int32, (128, WIDTH), 0)
    col = lax.broadcasted_iota(jnp.int32, (128, WIDTH), 1)
    pick = (row // HALF) * 128 + y * 32 + c * HALF + row % HALF
    one_hot = jnp.where(col == pick, 1.0, 0.0).astype(BF16)
    lhs[pl.ds(NZ, NZ)] = one_hot.reshape(NZ, HALF, WIDTH)

    clip = 2.0 * math.sqrt(NX * KF * WIDTH * WIDTH)
    norm = jnp.sqrt(norm_total(3, norm_z, NZ))
    factor = jnp.minimum(jnp.float32(1.0), clip / (norm + 1e-06))[0:1, 0:1]

    def times(ref):
        return (ref[...].astype(F32) * factor).astype(BF16)

    def column(k):
        return pl.multiple_of(lax.rem(z + NZ - ORDER[k], NZ) * LANES, LANES)

    for k in range(NZ):
        lhs[lax.rem(z + NZ - ORDER[k], NZ)] = times(gall.at[k, y, c])

    nt = (((1,), (1,)), ((), ()))

    def whole(b):
        arrived(gall.at[batch(b), :, oc], gf_rsem.at[b])
        first, count = BATCHES[b]
        for k in range(first, first + count):
            scaled[k] = times(gall.at[k])
        if b == 0:
            return
        n = b - 1
        both = lax.dot_general(
            lhs[...].reshape(256, WIDTH), scaled[pl.ds(2 * n, 2)].reshape(256, WIDTH), nt,
            preferred_element_type=F32,
        ).astype(BF16)
        for q in range(2):
            tile = both[:128, LANES * q:LANES * (q + 1)]
            left_s[n, :, q] = tile.reshape(NZ, HALF, LANES)
        lhs2[:, pl.ds(256 * n, 256)] = both[128:]
        for first, count in LEFT_RUNS:
            if first + count == b:
                runs = pl.ds(first, count)
                for d in ORDER[1:]:
                    remote(
                        left_s.at[runs, lax.rem(z + d, NZ)], out_r0.at[runs, z, c],
                        1, z_rsem.at[6], at_z(d),
                    ).start()

    def pass_roots(i, half):
        own = half.at[:, y, c]
        arrived(half.at[pl.ds(1, NZ - 1), y, c], z_rsem.at[4 + i])
        for d in (1, 3, 2):
            y_send(d, own, ry_rsem.at[i, d], 7)
        share(own, rf_rsem.at[i], 8)

    for b in range(5):
        for d in (1, 3, 2):
            here = gall.at[batch(b), from_y(d), c]
            arrived(here, gy_rsem.at[b, d])
            share(here, gf_rsem.at[b])
        if b:
            whole(b - 1)
    pass_roots(0, rh)
    whole(4)

    def gathered(i, half):
        for d in (1, 3, 2):
            here = half.at[:, from_y(d), c]
            arrived(here, ry_rsem.at[i, d])
            share(here, rf_rsem.at[i], 8)
        arrived(half.at[:, :, oc], rf_rsem.at[i])

    def o_sends(k):
        for d in ORDER[1:]:
            z_send(d, out_s.at[k], out_r[k].at[z, c], z_rsem.at[6 + k])
        out_r[k][z, c] = out_s[k, z]

    out_r0[:, z, c] = left_s[:, z]
    for n in range(4):
        g_cols = scaled[:, :, :, :, pl.ds(256 * n, 256)].reshape(WIDTH, 256)
        both = jnp.dot(lhs2[...], g_cols, preferred_element_type=F32).astype(BF16)
        out_s[1, :, :, pl.ds(256 * n, 256)] = both.reshape(NZ, HALF, 256)
    o_sends(1)
    arrived(lmine.at[pl.ds(0, NZ - 1)], z_rsem.at[5])
    for k in range(NZ):
        left[:, :, pl.ds(LANES * k, LANES)] = lmine[:, :, pl.ds(column(k), LANES)]
    for n in range(4):
        g_cols = scaled[:, :, :, :, pl.ds(256 * n, 256)].reshape(WIDTH, 256)
        app[:, pl.ds(256 * n, 256)] = jnp.dot(
            left[...].reshape(128, WIDTH), g_cols, preferred_element_type=F32
        ).astype(BF16)
    gathered(0, rh)
    unfold(rh, rfull)
    for n in range(4):
        r_cols = rfull[:, :, :, :, pl.ds(256 * n, 256)].reshape(WIDTH, 256)
        upd = jnp.dot(app[...], r_cols, preferred_element_type=F32).astype(BF16)
        out_s[2, :, :, pl.ds(256 * n, 256)] = upd.reshape(NZ, HALF, 256)
    o_sends(2)

    places, taken = [], []
    for s in range(SLOTS):
        place, count = jnp.int32(0), jnp.int32(0)
        for j in range(KF):
            hit = (owners[j] == c) & (ranks[j] == s)
            place = jnp.where(hit, j, place)
            count = jnp.where(hit, 1, count)
        places.append(place)
        taken.append(count)

    mix = (1.0 - STAT_DECAY) / WIDTH

    def finish_left():
        arrived(out_r0.at[:, pl.ds(0, NZ - 1), c], z_rsem.at[6])
        here = out_r0.at[:, :, c]
        remote(here, here, 5, o_rsem.at[0], at_c(1)).start()
        arrived(out_r0.at[:, :, oc], o_rsem.at[0])

    def left_gram(s, block):
        far = lax.rem(places[s] + NZ - block, NZ)
        pair = jnp.where(far > 4, NZ - far, jnp.maximum(far - 1, 0))
        second = jnp.where((far > 0) & (far < 5), 1, 0)
        return out_r0[pair, places[s], :, second]

    def finish(k):
        arrived(out_r[k].at[pl.ds(0, NZ - 1), c], z_rsem.at[6 + k])
        here = out_r[k].at[:, c]
        remote(here, here, 5, o_rsem.at[k], at_c(1)).start()
        arrived(out_r[k].at[:, oc], o_rsem.at[k])

    def stats(k, buf, out_ref):
        for s in range(SLOTS):
            if k == 0:
                gram = jnp.concatenate([left_gram(s, b) for b in range(NZ)], axis=-1).astype(F32)
            else:
                gram = out_r[k][places[s]].astype(F32)
            new = STAT_DECAY * buf[s] + mix * gram
            buf[s] = jnp.where(taken[s] > 0, new, buf[s])
        copy = pltpu.make_async_copy(buf, out_ref, fin_sem.at[k])
        copy.start()
        return copy

    local[4].wait()
    finish_left()
    done_left = stats(0, lst, nleft_ref)
    local[5].wait()
    finish(1)
    done_right = stats(1, rst, nright_ref)
    arrived(out_r2.at[pl.ds(0, NZ - 1), c], z_rsem.at[8])
    done_upd = pltpu.make_async_copy(out_r2.at[:, c], upd_ref.at[:, c], fin_sem.at[2])
    done_upd.start()
    remote(out_r2.at[:, c], upd_ref.at[:, c], 5, o_rsem.at[2], at_c(1)).start()
    arrived(upd_ref.at[:, oc], o_rsem.at[2])

    departed(gall.at[pl.ds(0, 5), :, 0], 0)
    departed(gall.at[pl.ds(0, 7), pl.ds(0, 2)], 1)
    departed(lpart.at[pl.ds(0, 7)], 9)
    departed(gall.at[pl.ds(0, 3)], 2)
    departed(gall.at[pl.ds(0, 4)], 3)
    departed(rpart.at[pl.ds(0, 7)], 6)
    departed(rh.at[pl.ds(0, 3)], 7)
    departed(rh.at[pl.ds(0, 4)], 8)
    departed(norm_w, 4)
    departed(gall.at[pl.ds(0, 3)], 5)
    for copy in (done_left, done_right, done_upd):
        copy.wait()


def hand_over(*refs):
    sems = refs[9]
    pieces = [(i, n) for i in range(3) for n in range(2)]
    halves = [refs[i].shape[0] // 2 for i in range(3)]

    def part(i, n):
        return pl.ds(n * halves[i], halves[i])

    loads = [
        pltpu.make_async_copy(
            refs[i].at[part(i, n)], refs[6 + i].at[part(i, n)], sems.at[0, i, n]
        )
        for i, n in pieces
    ]
    stores = [
        pltpu.make_async_copy(
            refs[6 + i].at[part(i, n)], refs[3 + i].at[part(i, n)], sems.at[1, i, n]
        )
        for i, n in pieces
    ]
    for copy in loads:
        copy.start()
    for load, store in zip(loads, stores):
        load.wait()
        store.start()
    for copy in stores:
        copy.wait()


def on_device(gradients, owner_lists, left_stats, right_stats, left_roots, right_roots):
    any_space = pl.BlockSpec(memory_space=pl.ANY)
    vmem, dma = pltpu.VMEM, pltpu.SemaphoreType.DMA
    stat_shape = (SLOTS, 2, HALF, WIDTH)
    new_left, new_right, updates = pl.pallas_call(
        kernel,
        out_shape=[
            jax.ShapeDtypeStruct(stat_shape, F32),
            jax.ShapeDtypeStruct(stat_shape, F32),
            jax.ShapeDtypeStruct((KF, 2, HALF, WIDTH), BF16),
        ],
        in_specs=[any_space] * 6,
        out_specs=[any_space] * 3,
        scratch_shapes=[
            pltpu.SMEM((1, KF), jnp.int32),
            vmem((KF, HALF, WIDTH), BF16),
            vmem((KF, HALF, WIDTH), BF16),
            vmem((KF, HALF, WIDTH), BF16),
            vmem((2, SLOTS, HALF, WIDTH), BF16),
            vmem((2, SLOTS, HALF, WIDTH), BF16),
            vmem((KF, HALF, WIDTH), BF16),
            vmem((KF, HALF, WEDGE * LANES), BF16),
            vmem((NZ, HALF, WIDTH), BF16),
            vmem((NZ, NY, 2, HALF, WIDTH), BF16),
            vmem((NZ, NY, 2, HALF, WEDGE * LANES), BF16),
            vmem((NZ, NY, 2, HALF, WIDTH), BF16),
            vmem((NZ, NY, 2, HALF, WIDTH), BF16),
            vmem((2 * NZ, HALF, WIDTH), BF16),
            vmem((128, WIDTH), BF16),
            vmem((NZ, HALF, WIDTH), BF16),
            vmem((128, WIDTH), BF16),
            vmem((NY, 8, 128), F32),
            vmem((NX, 8, 128), F32),
            vmem((2, 8, 128), F32),
            vmem((NZ, 8, 128), F32),
            vmem((14, 8, 128), F32),
            vmem((4, NZ, 2, HALF, LANES), BF16),
            vmem((3, NZ, HALF, WIDTH), BF16),
            vmem((4, KF, 2, 2, HALF, LANES), BF16),
            vmem((KF, 2, HALF, WIDTH), BF16),
            vmem((KF, 2, HALF, WIDTH), BF16),
            vmem(stat_shape, F32),
            vmem(stat_shape, F32),
            dma((6,)),
            dma((3,)),
            dma((9,)),
            dma((5, NY)),
            dma((1, NY)),
            dma((5,)),
            dma((1,)),
            dma((4,)),
            dma((3,)),
            dma((3,)),
            dma((10,)),
        ],
        compiler_params=pltpu.CompilerParams(
            collective_id=0, has_side_effects=True, vmem_limit_bytes=60 * 2**20
        ),
    )(
        owner_lists,
        gradients.reshape(KF, 2, HALF, WIDTH),
        left_stats.reshape(stat_shape),
        right_stats.reshape(stat_shape),
        left_roots.reshape(stat_shape),
        right_roots.reshape(stat_shape),
    )
    new_left, new_right, updates = pl.pallas_call(
        hand_over,
        out_shape=[
            jax.ShapeDtypeStruct(stat_shape, F32),
            jax.ShapeDtypeStruct(stat_shape, F32),
            jax.ShapeDtypeStruct((KF, 2, HALF, WIDTH), BF16),
        ],
        in_specs=[any_space] * 3,
        out_specs=[any_space] * 3,
        scratch_shapes=[
            vmem(stat_shape, F32),
            vmem(stat_shape, F32),
            vmem((KF, 2, HALF, WIDTH), BF16),
            dma((2, 3, 2)),
        ],
        compiler_params=pltpu.CompilerParams(vmem_limit_bytes=60 * 2**20),
    )(new_left, new_right, updates)
    full = (1, 1, SLOTS, 2 * HALF, WIDTH)
    return (
        new_left.reshape(full),
        new_right.reshape(full),
        updates.reshape(KF, 2 * HALF, WIDTH),
    )


def solution(mesh):
    placed = (
        P("dp", "fsdp", "tensor", None),
        P("fsdp", None),
        P("dp", "fsdp", None, "tensor", None),
        P("dp", "fsdp", None, "tensor", None),
        P("dp", "fsdp", None, "tensor", None),
        P("dp", "fsdp", None, "tensor", None),
    )
    return jax.shard_map(
        on_device,
        mesh=mesh,
        in_specs=placed,
        out_specs=(
            P("dp", "fsdp", None, "tensor", None),
            P("dp", "fsdp", None, "tensor", None),
            P("fsdp", "tensor", None),
        ),
        check_vma=False,
    )
```

```python
import functools
import math

import jax
import jax.numpy as jnp
from jax import lax
from jax.experimental import pallas as pl
from jax.experimental.pallas import tpu as pltpu
from jax.sharding import PartitionSpec as P

STAT_DECAY = 0.9
MESH = pl.DeviceIdType.MESH
NZ = 8
NY = 4
NX = 4
HALF = 16
WIDTH = 1024
LANES = 128
WEDGE = 5
KF = 8
SLOTS = 6
ORDER = (0, 1, 7, 2, 6, 3, 5, 4)
BATCHES = ((0, 1), (1, 2), (3, 2), (5, 2), (7, 1))
LEFT_RUNS = ((0, 1), (1, 1), (2, 1), (3, 1))
BF16 = jnp.bfloat16
F32 = jnp.float32


def kernel(
    owner_hbm, grad_ref, lstat_ref, rstat_ref, lroot_ref, rroot_ref,
    nleft_ref, nright_ref, upd_ref,
    owner_ref, own_g, got_g, part, lboth, rboth, lpart, rpart, lmine,
    gall, rh, scaled, rfull, lhs, lhs2, left, app,
    norm_y, norm_x, norm_c, norm_z, norm_w,
    left_s, out_s, out_r0, out_r1, out_r2, lst, rst,
    loc_sem, c_rsem, z_rsem, gy_rsem, ry_rsem, gf_rsem, rf_rsem, n_rsem, o_rsem, fin_sem, s_sem,
):
    out_r = (out_r0, out_r1, out_r2)
    c = lax.axis_index("dp")
    x = lax.axis_index("fsdp")
    t = lax.axis_index("tensor")
    z, y = t // NY, t % NY
    oc = 1 - c

    def at_z(d):
        return {"tensor": lax.rem(z + d, NZ) * NY + y}

    def at_y(d):
        return {"tensor": z * NY + lax.rem(y + d, NY)}

    def at_x(d):
        return {"fsdp": lax.rem(x + d, NX)}

    def at_c(d):
        return {"dp": oc}

    def remote(src, dst, ssem, rsem, device):
        return pltpu.make_async_remote_copy(
            src_ref=src, dst_ref=dst, send_sem=s_sem.at[ssem], recv_sem=rsem,
            device_id=device, device_id_type=MESH,
        )

    def arrived(ref, rsem):
        remote(ref, ref, 0, rsem, at_c(1)).wait_recv()

    def departed(ref, ssem):
        remote(ref, ref, ssem, fin_sem.at[0], at_c(1)).wait_send()

    local = [
        pltpu.make_async_copy(grad_ref.at[:, c], own_g, loc_sem.at[0]),
        pltpu.make_async_copy(rroot_ref.at[:, c], rboth.at[c], loc_sem.at[1]),
        pltpu.make_async_copy(lroot_ref.at[:, c], lboth.at[c], loc_sem.at[2]),
        pltpu.make_async_copy(owner_hbm, owner_ref, loc_sem.at[3]),
        pltpu.make_async_copy(lstat_ref, lst, loc_sem.at[4]),
        pltpu.make_async_copy(rstat_ref, rst, loc_sem.at[5]),
    ]
    for copy in local[:4]:
        copy.start()

    peers = (
        [at_z(d) for d in range(1, NZ)]
        + [at_y(d) for d in range(1, NY)]
        + [at_x(d) for d in range(1, NX)]
        + [at_c(1)]
    )
    barrier = pltpu.get_barrier_semaphore()
    for peer in peers:
        pl.semaphore_signal(barrier, inc=1, device_id=peer, device_id_type=MESH)
    pl.semaphore_wait(barrier, len(peers))

    remote(grad_ref.at[:, oc], got_g, 0, c_rsem.at[0], at_c(1)).start()
    remote(rroot_ref.at[:, oc], rboth.at[c], 0, c_rsem.at[1], at_c(1)).start()
    remote(lroot_ref.at[:, oc], lboth.at[c], 0, c_rsem.at[2], at_c(1)).start()

    local[0].wait()
    arrived(got_g, c_rsem.at[0])

    def z_send(d, src, dst, rsem, ssem=1):
        remote(src.at[lax.rem(z + d, NZ)], dst, ssem, rsem, at_z(d)).start()

    def y_send(d, ref, rsem, ssem=2):
        remote(ref, ref, ssem, rsem, at_y(d)).start()

    def share(ref, rsem, ssem=3):
        remote(ref, ref, ssem, rsem, at_c(1)).start()

    def batch(b):
        return pl.ds(*BATCHES[b])

    def from_y(d):
        return lax.rem(y + NY - d, NY)

    def pass_on(b):
        own = gall.at[batch(b), y, c]
        for d in (1, 3, 2):
            y_send(d, own, gy_rsem.at[b, d])
        share(own, gf_rsem.at[b])

    def wave(b):
        first, count = BATCHES[b]
        for k in range(first, first + count):
            z_send(ORDER[k], part, gall.at[k, y, c], z_rsem.at[b - 1])

    squares = jnp.zeros((HALF, WIDTH), F32)
    for k, d in enumerate(ORDER):
        j = lax.rem(z + d, NZ)
        total = own_g[j].astype(F32) + got_g[j].astype(F32)
        squares += total * total
        if d:
            part[j] = total.astype(BF16)
        else:
            gall[0, y, c] = total.astype(BF16)
        if k == 2:
            wave(1)

    def norm_sends(k, buf, here, at, count):
        for d in range(1, count):
            remote(buf.at[here], buf.at[here], 4, n_rsem.at[k], at(d)).start()

    def norm_total(k, buf, count):
        arrived(buf.at[pl.ds(0, count - 1)], n_rsem.at[k])
        return jnp.sum(buf[...], axis=0)

    norm_y[y] = jnp.full((8, 128), jnp.sum(squares), F32)
    norm_sends(0, norm_y, y, at_y, NY)
    pass_on(0)
    for copy in local[4:]:
        copy.start()

    local[3].wait()
    owners = [owner_ref[0, j] for j in range(KF)]
    ranks = []
    for j in range(KF):
        rank = jnp.int32(0)
        for i in range(j):
            rank += jnp.where(owners[i] == owners[j], 1, 0).astype(jnp.int32)
        ranks.append(jnp.minimum(rank, SLOTS - 1))

    def wedge(both, parts, half):
        for j in range(KF):
            for m in range(WEDGE):
                there = pl.multiple_of(lax.rem(z + m, NZ) * LANES, LANES)
                parts[j, :, pl.ds(LANES * m, LANES)] = both[
                    owners[j], ranks[j], :, pl.ds(there, LANES)
                ]
        half[0, y, c] = parts[z]

    def wedge_sends(parts, half, rsem, order=ORDER[1:]):
        for d in order:
            z_send(d, parts, half.at[NZ - d, y, c], rsem, 6)

    def unfold(half, full):
        for k in range(NZ):
            zz = lax.rem(z + k, NZ)
            here = pl.multiple_of(zz * LANES, LANES)
            for m in range(WEDGE):
                tile = half[k, :, :, :, pl.ds(LANES * m, LANES)]
                ww = lax.rem(z + k + m, NZ)
                there = pl.multiple_of(ww * LANES, LANES)
                full[zz, :, :, :, pl.ds(there, LANES)] = tile
                if m in (1, 2, 3):
                    turned = tile.reshape(LANES, LANES).T
                    full[ww, :, :, :, pl.ds(here, LANES)] = turned.reshape(NY, 2, HALF, LANES)

    local[1].wait()
    arrived(rboth.at[c], c_rsem.at[1])
    wedge(rboth, rpart, rh)
    local[2].wait()
    arrived(lboth.at[c], c_rsem.at[2])
    for j in range(KF):
        lpart[j] = lboth[owners[j], ranks[j]]
    lmine[z] = lpart[z]

    wave(2)
    wave(3)
    arrived(gall.at[batch(1), y, c], z_rsem.at[0])
    pass_on(1)
    norm_x[x] = norm_total(0, norm_y, NY)
    norm_sends(1, norm_x, x, at_x, NX)
    wave(4)
    arrived(gall.at[batch(2), y, c], z_rsem.at[1])
    pass_on(2)
    norm_c[c] = norm_total(1, norm_x, NX)
    norm_sends(2, norm_c, c, at_c, 2)
    norm_z[z] = norm_total(2, norm_c, 2)
    norm_sends(3, norm_z, z, at_z, NZ)
    wedge_sends(rpart, rh, z_rsem.at[4])
    arrived(gall.at[batch(3), y, c], z_rsem.at[2])
    pass_on(3)
    arrived(gall.at[batch(4), y, c], z_rsem.at[3])
    pass_on(4)
    for d in ORDER[1:]:
        z_send(d, lpart, lmine.at[z], z_rsem.at[5], 9)

    row = lax.broadcasted_iota(jnp.int32, (128, WIDTH), 0)
    col = lax.broadcasted_iota(jnp.int32, (128, WIDTH), 1)
    pick = (row // HALF) * 128 + y * 32 + c * HALF + row % HALF
    one_hot = jnp.where(col == pick, 1.0, 0.0).astype(BF16)
    lhs[pl.ds(NZ, NZ)] = one_hot.reshape(NZ, HALF, WIDTH)

    clip = 2.0 * math.sqrt(NX * KF * WIDTH * WIDTH)
    norm = jnp.sqrt(norm_total(3, norm_z, NZ))
    factor = jnp.minimum(jnp.float32(1.0), clip / (norm + 1e-06))[0:1, 0:1]

    def times(ref):
        return (ref[...].astype(F32) * factor).astype(BF16)

    def column(k):
        return pl.multiple_of(lax.rem(z + NZ - ORDER[k], NZ) * LANES, LANES)

    for k in range(NZ):
        lhs[lax.rem(z + NZ - ORDER[k], NZ)] = times(gall.at[k, y, c])

    nt = (((1,), (1,)), ((), ()))

    def whole(b):
        arrived(gall.at[batch(b), :, oc], gf_rsem.at[b])
        first, count = BATCHES[b]
        for k in range(first, first + count):
            scaled[k] = times(gall.at[k])
        if b == 0:
            return
        n = b - 1
        both = lax.dot_general(
            lhs[...].reshape(256, WIDTH), scaled[pl.ds(2 * n, 2)].reshape(256, WIDTH), nt,
            preferred_element_type=F32,
        ).astype(BF16)
        for q in range(2):
            tile = both[:128, LANES * q:LANES * (q + 1)]
            left_s[n, :, q] = tile.reshape(NZ, HALF, LANES)
        lhs2[:, pl.ds(256 * n, 256)] = both[128:]
        for first, count in LEFT_RUNS:
            if first + count == b:
                runs = pl.ds(first, count)
                for d in ORDER[1:]:
                    remote(
                        left_s.at[runs, lax.rem(z + d, NZ)], out_r0.at[runs, z, c],
                        1, z_rsem.at[6], at_z(d),
                    ).start()

    def pass_roots(i, half):
        own = half.at[:, y, c]
        arrived(half.at[pl.ds(1, NZ - 1), y, c], z_rsem.at[4 + i])
        for d in (1, 3, 2):
            y_send(d, own, ry_rsem.at[i, d], 7)
        share(own, rf_rsem.at[i], 8)

    for b in range(5):
        for d in (1, 3, 2):
            here = gall.at[batch(b), from_y(d), c]
            arrived(here, gy_rsem.at[b, d])
            share(here, gf_rsem.at[b])
        if b:
            whole(b - 1)
    pass_roots(0, rh)
    whole(4)

    def gathered(i, half):
        for d in (1, 3, 2):
            here = half.at[:, from_y(d), c]
            arrived(here, ry_rsem.at[i, d])
            share(here, rf_rsem.at[i], 8)
        arrived(half.at[:, :, oc], rf_rsem.at[i])

    def o_sends(k):
        for d in ORDER[1:]:
            z_send(d, out_s.at[k], out_r[k].at[z, c], z_rsem.at[6 + k])
        out_r[k][z, c] = out_s[k, z]

    out_r0[:, z, c] = left_s[:, z]
    for n in range(4):
        g_cols = scaled[:, :, :, :, pl.ds(256 * n, 256)].reshape(WIDTH, 256)
        both = jnp.dot(lhs2[...], g_cols, preferred_element_type=F32).astype(BF16)
        out_s[1, :, :, pl.ds(256 * n, 256)] = both.reshape(NZ, HALF, 256)
    o_sends(1)
    arrived(lmine.at[pl.ds(0, NZ - 1)], z_rsem.at[5])
    for k in range(NZ):
        left[:, :, pl.ds(LANES * k, LANES)] = lmine[:, :, pl.ds(column(k), LANES)]
    for n in range(4):
        g_cols = scaled[:, :, :, :, pl.ds(256 * n, 256)].reshape(WIDTH, 256)
        app[:, pl.ds(256 * n, 256)] = jnp.dot(
            left[...].reshape(128, WIDTH), g_cols, preferred_element_type=F32
        ).astype(BF16)
    gathered(0, rh)
    unfold(rh, rfull)
    for n in range(4):
        r_cols = rfull[:, :, :, :, pl.ds(256 * n, 256)].reshape(WIDTH, 256)
        upd = jnp.dot(app[...], r_cols, preferred_element_type=F32).astype(BF16)
        out_s[2, :, :, pl.ds(256 * n, 256)] = upd.reshape(NZ, HALF, 256)
        if n % 2:
            run = pl.ds(256 * (n - 1), 512)
            for d in ORDER[1:]:
                remote(
                    out_s.at[2, lax.rem(z + d, NZ), :, run], out_r2.at[z, c, :, run],
                    1, z_rsem.at[8], at_z(d),
                ).start()
    out_r2[z, c] = out_s[2, z]

    places, taken = [], []
    for s in range(SLOTS):
        place, count = jnp.int32(0), jnp.int32(0)
        for j in range(KF):
            hit = (owners[j] == c) & (ranks[j] == s)
            place = jnp.where(hit, j, place)
            count = jnp.where(hit, 1, count)
        places.append(place)
        taken.append(count)

    mix = (1.0 - STAT_DECAY) / WIDTH

    def finish_left():
        arrived(out_r0.at[:, pl.ds(0, NZ - 1), c], z_rsem.at[6])
        here = out_r0.at[:, :, c]
        remote(here, here, 5, o_rsem.at[0], at_c(1)).start()
        arrived(out_r0.at[:, :, oc], o_rsem.at[0])

    def left_gram(s, block):
        far = lax.rem(places[s] + NZ - block, NZ)
        pair = jnp.where(far > 4, NZ - far, jnp.maximum(far - 1, 0))
        second = jnp.where((far > 0) & (far < 5), 1, 0)
        return out_r0[pair, places[s], :, second]

    def finish(k):
        arrived(out_r[k].at[pl.ds(0, NZ - 1), c], z_rsem.at[6 + k])
        here = out_r[k].at[:, c]
        remote(here, here, 5, o_rsem.at[k], at_c(1)).start()
        arrived(out_r[k].at[:, oc], o_rsem.at[k])

    def stats(k, buf, out_ref):
        for s in range(SLOTS):
            if k == 0:
                gram = jnp.concatenate([left_gram(s, b) for b in range(NZ)], axis=-1).astype(F32)
            else:
                gram = out_r[k][places[s]].astype(F32)
            new = STAT_DECAY * buf[s] + mix * gram
            buf[s] = jnp.where(taken[s] > 0, new, buf[s])
        copy = pltpu.make_async_copy(buf, out_ref, fin_sem.at[k])
        copy.start()
        return copy

    local[4].wait()
    finish_left()
    done_left = stats(0, lst, nleft_ref)
    local[5].wait()
    finish(1)
    done_right = stats(1, rst, nright_ref)
    arrived(out_r2.at[pl.ds(0, NZ - 1), c], z_rsem.at[8])
    done_upd = pltpu.make_async_copy(out_r2.at[:, c], upd_ref.at[:, c], fin_sem.at[2])
    done_upd.start()
    remote(out_r2.at[:, c], upd_ref.at[:, c], 5, o_rsem.at[2], at_c(1)).start()
    arrived(upd_ref.at[:, oc], o_rsem.at[2])

    departed(gall.at[pl.ds(0, 5), :, 0], 0)
    departed(gall.at[pl.ds(0, 7), pl.ds(0, 2)], 1)
    departed(lpart.at[pl.ds(0, 7)], 9)
    departed(gall.at[pl.ds(0, 3)], 2)
    departed(gall.at[pl.ds(0, 4)], 3)
    departed(rpart.at[pl.ds(0, 7)], 6)
    departed(rh.at[pl.ds(0, 3)], 7)
    departed(rh.at[pl.ds(0, 4)], 8)
    departed(norm_w, 4)
    departed(gall.at[pl.ds(0, 3)], 5)
    for copy in (done_left, done_right, done_upd):
        copy.wait()


def hand_over(*refs):
    sems = refs[9]
    pieces = [(i, n) for i in range(3) for n in range(2)]
    halves = [refs[i].shape[0] // 2 for i in range(3)]

    def part(i, n):
        return pl.ds(n * halves[i], halves[i])

    loads = [
        pltpu.make_async_copy(
            refs[i].at[part(i, n)], refs[6 + i].at[part(i, n)], sems.at[0, i, n]
        )
        for i, n in pieces
    ]
    stores = [
        pltpu.make_async_copy(
            refs[6 + i].at[part(i, n)], refs[3 + i].at[part(i, n)], sems.at[1, i, n]
        )
        for i, n in pieces
    ]
    for copy in loads:
        copy.start()
    for load, store in zip(loads, stores):
        load.wait()
        store.start()
    for copy in stores:
        copy.wait()


def on_device(gradients, owner_lists, left_stats, right_stats, left_roots, right_roots):
    any_space = pl.BlockSpec(memory_space=pl.ANY)
    vmem, dma = pltpu.VMEM, pltpu.SemaphoreType.DMA
    stat_shape = (SLOTS, 2, HALF, WIDTH)
    new_left, new_right, updates = pl.pallas_call(
        kernel,
        out_shape=[
            jax.ShapeDtypeStruct(stat_shape, F32),
            jax.ShapeDtypeStruct(stat_shape, F32),
            jax.ShapeDtypeStruct((KF, 2, HALF, WIDTH), BF16),
        ],
        in_specs=[any_space] * 6,
        out_specs=[any_space] * 3,
        scratch_shapes=[
            pltpu.SMEM((1, KF), jnp.int32),
            vmem((KF, HALF, WIDTH), BF16),
            vmem((KF, HALF, WIDTH), BF16),
            vmem((KF, HALF, WIDTH), BF16),
            vmem((2, SLOTS, HALF, WIDTH), BF16),
            vmem((2, SLOTS, HALF, WIDTH), BF16),
            vmem((KF, HALF, WIDTH), BF16),
            vmem((KF, HALF, WEDGE * LANES), BF16),
            vmem((NZ, HALF, WIDTH), BF16),
            vmem((NZ, NY, 2, HALF, WIDTH), BF16),
            vmem((NZ, NY, 2, HALF, WEDGE * LANES), BF16),
            vmem((NZ, NY, 2, HALF, WIDTH), BF16),
            vmem((NZ, NY, 2, HALF, WIDTH), BF16),
            vmem((2 * NZ, HALF, WIDTH), BF16),
            vmem((128, WIDTH), BF16),
            vmem((NZ, HALF, WIDTH), BF16),
            vmem((128, WIDTH), BF16),
            vmem((NY, 8, 128), F32),
            vmem((NX, 8, 128), F32),
            vmem((2, 8, 128), F32),
            vmem((NZ, 8, 128), F32),
            vmem((14, 8, 128), F32),
            vmem((4, NZ, 2, HALF, LANES), BF16),
            vmem((3, NZ, HALF, WIDTH), BF16),
            vmem((4, KF, 2, 2, HALF, LANES), BF16),
            vmem((KF, 2, HALF, WIDTH), BF16),
            vmem((KF, 2, HALF, WIDTH), BF16),
            vmem(stat_shape, F32),
            vmem(stat_shape, F32),
            dma((6,)),
            dma((3,)),
            dma((9,)),
            dma((5, NY)),
            dma((1, NY)),
            dma((5,)),
            dma((1,)),
            dma((4,)),
            dma((3,)),
            dma((3,)),
            dma((10,)),
        ],
        compiler_params=pltpu.CompilerParams(
            collective_id=0, has_side_effects=True, vmem_limit_bytes=60 * 2**20
        ),
    )(
        owner_lists,
        gradients.reshape(KF, 2, HALF, WIDTH),
        left_stats.reshape(stat_shape),
        right_stats.reshape(stat_shape),
        left_roots.reshape(stat_shape),
        right_roots.reshape(stat_shape),
    )
    new_left, new_right, updates = pl.pallas_call(
        hand_over,
        out_shape=[
            jax.ShapeDtypeStruct(stat_shape, F32),
            jax.ShapeDtypeStruct(stat_shape, F32),
            jax.ShapeDtypeStruct((KF, 2, HALF, WIDTH), BF16),
        ],
        in_specs=[any_space] * 3,
        out_specs=[any_space] * 3,
        scratch_shapes=[
            vmem(stat_shape, F32),
            vmem(stat_shape, F32),
            vmem((KF, 2, HALF, WIDTH), BF16),
            dma((2, 3, 2)),
        ],
        compiler_params=pltpu.CompilerParams(vmem_limit_bytes=60 * 2**20),
    )(new_left, new_right, updates)
    full = (1, 1, SLOTS, 2 * HALF, WIDTH)
    return (
        new_left.reshape(full),
        new_right.reshape(full),
        updates.reshape(KF, 2 * HALF, WIDTH),
    )


def solution(mesh):
    placed = (
        P("dp", "fsdp", "tensor", None),
        P("fsdp", None),
        P("dp", "fsdp", None, "tensor", None),
        P("dp", "fsdp", None, "tensor", None),
        P("dp", "fsdp", None, "tensor", None),
        P("dp", "fsdp", None, "tensor", None),
    )
    return jax.shard_map(
        on_device,
        mesh=mesh,
        in_specs=placed,
        out_specs=(
            P("dp", "fsdp", None, "tensor", None),
            P("dp", "fsdp", None, "tensor", None),
            P("fsdp", "tensor", None),
        ),
        check_vma=False,
    )
```
